512 devices in a mesh: node: 32 (over x, y), chan: 16 (over z, core).
Axes of the slice: x: 4, y: 8, z: 8, core: 2. Of those that a mesh axis runs over, the one named last changes fastest.
Arguments:
- features: bfloat16 [57344, 1024], P('node', 'chan'), may hold values from -0.046875 to 0.046875
- weight: bfloat16 [1024, 1024], P('node', 'chan'), may hold values from -0.375 to 0.375
- pre_clean: bfloat16 [57344, 1024], P('node', 'chan'), may hold values from -6 to 6
- pre_corrupt: bfloat16 [57344, 1024], P('node', 'chan'), may hold values from -6 to 6
- grad_clean: bfloat16 [57344, 1024], P('node', 'chan'), may hold values from -6 to 6
- grad_corrupt: bfloat16 [57344, 1024], P('node', 'chan'), may hold values from -6 to 6
- slopes: float32 [1024], P('chan'), may hold values from 0.05 to 0.5
- adj_vals: bfloat16 [448, 5, 128, 128], P('node'), may hold values from 0 to 0.07861328
- adj_cols: int32 [448, 5], P('node'), may hold values from 0 to 447, as said below
- adj_count: int32 [448], P('node'), may hold values from 1 to 5, as said below
- shuffle_from: int32 [448], replicated, may hold values from 0 to 447, as said below
Outputs:
- grad_weight: float32 [1024, 1024], P('node', 'chan')
- grad_features: bfloat16 [57344, 1024], P('node', 'chan')
The draws below stay inside these ranges and needn't reach their ends.
Inputs may be any that keep to these rules, and one draw needn't show every extreme that they name: `adj_cols`: entry [b, k] is a block within 2 of b, and entry [b, 0] is b itself. Slots k < adj_count[b] of row block b hold edge tiles; the other slots are padding and are not read. `shuffle_from`: A permutation of the blocks. The 14 blocks of one index of node take their rows from exactly 14 distinct indices of node, 1 block from each; among these are the index just after it and the index 16 away, counted round.
All inputs are finite; a program needn't handle non-finite values.
Results may differ from the reference program's by a relative error of at most 0.023.
Values may be sent and summed in bfloat16 or wider, within the bound.
A program may use at most 64 MiB of HBM per device.

```python
import math
import jax
import jax.numpy as jnp
from jax import lax

F = 1024
TB = 128
BAND = 2
KMAX = 5
BLK_DEV = 14
CAP = 1
NBLK = 448
NODES = 57344
N_CHAN = 16


def draw_adj_cols(key, part):
    scores = jax.random.randint(key, (NBLK, 2 * BAND), 0, 1 << 20) * (2 * BAND) + jnp.arange(2 * BAND)[None, :]
    shuffled = jnp.argsort(scores, axis=1)
    nonzero = jnp.concatenate([jnp.arange(-BAND, 0), jnp.arange(1, BAND + 1)])
    offsets = jnp.concatenate([jnp.zeros((NBLK, 1), jnp.int32), nonzero[shuffled].astype(jnp.int32)], axis=1)
    columns = jnp.arange(NBLK)[:, None] + offsets
    columns = jnp.where(columns < 0, -columns, columns)
    columns = jnp.where(columns > NBLK - 1, 2 * (NBLK - 1) - columns, columns)
    return columns.astype(jnp.int32)


def draw_adj_count(key, part):
    dev_count = NBLK // BLK_DEV
    key_one, key_two, key_three = jax.random.split(key, 3)
    largest = jax.random.randint(key_one, (dev_count,), 1, KMAX + 1)
    largest_rows = jnp.repeat(largest, BLK_DEV)
    picked = jax.random.randint(key_two, (NBLK,), 0, 1 << 20)
    counts = 1 + picked % largest_rows
    full_row = jax.random.randint(key_three, (), 0, NBLK)
    counts = jnp.where(jnp.arange(NBLK) == full_row, KMAX, counts)
    return counts.astype(jnp.int32)


def draw_shuffle_from(key, part):
    key = jax.random.fold_in(key, 7)
    dev_count = NBLK // BLK_DEV
    groups = BLK_DEV // CAP
    key_one, key_two, key_three = jax.random.split(key, 3)
    values = jnp.arange(dev_count - 2)
    rest = jnp.where(values == 0, 0, values + 1)
    rest = jnp.where((values > 0) & (rest >= dev_count // 2), rest + 1, rest)
    rest = rest[jax.random.permutation(key_one, dev_count - 2)]
    shifts = jnp.concatenate([jnp.array([1, dev_count // 2], jnp.int32), rest.astype(jnp.int32)])[:groups]
    base = jax.random.permutation(key_two, BLK_DEV)
    scores = jax.random.randint(key_three, (dev_count, BLK_DEV), 0, 1 << 20) * BLK_DEV + jnp.arange(BLK_DEV)[None, :]
    order = jnp.argsort(scores, axis=1)
    device_of = jnp.arange(NBLK) // BLK_DEV
    position = jnp.arange(NBLK) % BLK_DEV
    slot = order[device_of, position]
    source_dev = (device_of + shifts[slot // CAP]) % dev_count
    return (source_dev * BLK_DEV + base[slot]).astype(jnp.int32)


def raised(result, key, source, target, shards_of, factor):
    def block_of(dim):
        return (jnp.arange(result.shape[dim]) // (result.shape[dim] // shards_of)).reshape((-1,) + (1,) * (result.ndim - 1 - dim))

    near = jax.random.permutation(key, shards_of)[block_of(target)]
    other_side = (block_of(target) + shards_of // 2) % shards_of
    return jnp.where((block_of(source) == near) | (block_of(source) == other_side), factor * result, result)


def level_of(own_key, extent, cuts, smallest, high):
    gain = 1.0
    for axis_at, shards_of in cuts:
        heights = jax.random.uniform(jax.random.fold_in(jax.random.fold_in(own_key, 6), axis_at), (shards_of,), jnp.float32, smallest / len(cuts), high / len(cuts))
        gain = gain * jnp.repeat(jnp.exp(heights), extent[axis_at] // shards_of).reshape((-1,) + (1,) * (len(extent) - 1 - axis_at))
    return gain


def normal_values(stream_key, shape, scale, reach, shards=(), held_as=jnp.bfloat16):
    level = level_of(stream_key, shape, shards, -0.22, 0.18) if shards else 1.0
    entries = jax.random.normal(stream_key, shape, jnp.float32) * scale * level
    return jnp.minimum(jnp.maximum(entries, -reach), reach).astype(held_as)


def bell_draw_with(rng, dims, deviation, limit, cuts, heavy, kind=jnp.bfloat16):
    drawn = deviation * jax.random.normal(rng, dims, jnp.float32)
    if cuts:
        drawn = drawn * level_of(rng, dims, cuts, -0.22, 0.18)
    return jnp.clip(raised(drawn, jax.random.fold_in(rng, 3), *heavy), -limit, limit).astype(kind)


def setup_inputs(seed: int = 0) -> dict:
    arg_keys = jax.random.split(jax.random.key(seed), 12)
    features = bell_draw_with(arg_keys[0], (NODES, F), (NODES ** -0.5), 0.046875, ((0, 32), (1, 16)), (0, 1, 32, 2.75))
    weight = bell_draw_with(arg_keys[1], (F, F), F ** -0.5, 0.375, ((0, 32), (1, 16)), (1, 0, 32, 2.75))
    pre_clean = normal_values(arg_keys[2], (NODES, F), 1.0, 6.0, ((0, 32), (1, 16)))
    pre_corrupt = normal_values(arg_keys[3], (NODES, F), 1.0, 6.0, ((0, 32), (1, 16)))
    grad_clean = normal_values(arg_keys[4], (NODES, F), 1.0, 6.0, ((0, 32), (1, 16)))
    grad_corrupt = normal_values(arg_keys[5], (NODES, F), 1.0, 6.0, ((0, 32), (1, 16)))
    slopes = jnp.clip(jnp.exp(math.log(0.5) - 2.3025851 * jax.random.uniform(arg_keys[6], (F,), jnp.float32) ** level_of(arg_keys[6], (F,), ((0, 16),), -0.2, 0.2)), 0.05, 0.5)
    adj_vals = jnp.clip(0.07861328 * jax.random.uniform(arg_keys[7], (NBLK, KMAX, TB, TB), jnp.float32) ** level_of(arg_keys[7], (NBLK, KMAX, TB, TB), ((0, 32),), -0.2, 0.2), 0.0, 0.07861328).astype(jnp.bfloat16)
    adj_cols = draw_adj_cols(jax.random.fold_in(arg_keys[11], 71), 0)
    adj_count = draw_adj_count(jax.random.fold_in(arg_keys[11], 71), 0)
    shuffle_from = draw_shuffle_from(jax.random.fold_in(arg_keys[11], 71), 0)
    return dict(features=features, weight=weight, pre_clean=pre_clean, pre_corrupt=pre_corrupt, grad_clean=grad_clean, grad_corrupt=grad_corrupt, slopes=slopes, adj_vals=adj_vals, adj_cols=adj_cols, adj_count=adj_count, shuffle_from=shuffle_from)


def local_grad(grad_part, pre_part, slopes):
    factor = jnp.where(pre_part > 0, 1.0, slopes[None, :])
    return (grad_part.astype(jnp.float32) * factor).astype(jnp.bfloat16)

def reference(features, weight, pre_clean, pre_corrupt, grad_clean, grad_corrupt, slopes, adj_vals, adj_cols, adj_count, shuffle_from):
    d_clean = local_grad(grad_clean, pre_clean, slopes)
    d_corrupt = local_grad(grad_corrupt, pre_corrupt, slopes)
    block_count = adj_cols.shape[0]
    tile_rows = adj_vals.shape[2]
    stacked = jnp.concatenate([d_clean, d_corrupt], axis=1).reshape(block_count, tile_rows, 2 * F)

    def one_block(summed, inputs):
        tile_vals, columns, tile_count, rhs_block = inputs
        contrib = jnp.einsum('kpq,pc->kqc', tile_vals.astype(jnp.float32), rhs_block.astype(jnp.float32))
        live_mask = (jnp.arange(tile_vals.shape[0], dtype=jnp.int32) < tile_count).astype(jnp.float32)
        return (summed.at[columns].add(contrib * live_mask[:, None, None]), None)
    start_sum = jnp.zeros((block_count, tile_rows, 2 * F), jnp.float32)
    summed, _ = lax.scan(one_block, start_sum, (adj_vals, adj_cols, adj_count, stacked))
    backprop = summed.astype(jnp.bfloat16)
    back_clean = backprop[:, :, :F].reshape(block_count * tile_rows, F)
    back_corrupt = backprop[:, :, F:]
    unshuffled = jnp.zeros_like(back_corrupt).at[shuffle_from].set(back_corrupt).reshape(block_count * tile_rows, F)
    grad_weight = jnp.dot(features.T, back_clean, preferred_element_type=jnp.float32) + jnp.dot(features.T, unshuffled, preferred_element_type=jnp.float32)
    chan_width = F // N_CHAN

    def add_partial(block_index, running):
        start_col = (block_index * chan_width).astype(jnp.int32)
        first_part = lax.dynamic_slice_in_dim(back_clean, start_col, chan_width, 1)
        second_part = lax.dynamic_slice_in_dim(unshuffled, start_col, chan_width, 1)
        weight_part = lax.dynamic_slice_in_dim(weight, start_col, chan_width, 1)
        partial_value = jnp.dot(first_part, weight_part.T, preferred_element_type=jnp.float32) + jnp.dot(second_part, weight_part.T, preferred_element_type=jnp.float32)
        rounded = lax.optimization_barrier(partial_value.astype(jnp.bfloat16))
        return running + rounded.astype(jnp.float32)
    running = lax.fori_loop(0, N_CHAN, add_partial, jnp.zeros((block_count * tile_rows, F), jnp.float32))
    return (grad_weight, running.astype(jnp.bfloat16))
```

```python
import functools

import jax
import jax.numpy as jnp
from jax import lax
from jax.experimental import pallas as pl
from jax.experimental.pallas import tpu as pltpu
from jax.sharding import PartitionSpec as P

MESH = pl.DeviceIdType.MESH
BF16 = jnp.bfloat16
F32 = jnp.float32


def band_kernel(
    cols_ref, count_ref, gc_ref, pc_ref, gx_ref, px_ref, slope_ref, adj_ref,
    main_ref, before_ref, after_ref, acc,
):
    blocks, slots, rows, _ = adj_ref.shape
    reach = (slots - 1) // 2
    base = lax.axis_index("node") * blocks - reach
    acc[...] = jnp.zeros_like(acc)
    slope = slope_ref[...]
    spare = blocks + 2 * reach
    for b in range(blocks):
        here = slice(b * rows, (b + 1) * rows)

        def grad(g_ref, p_ref):
            g = g_ref[:, here].astype(F32)
            return jnp.where(p_ref[:, here].astype(F32) > 0, g, g * slope).astype(BF16)

        d = jnp.concatenate([grad(gc_ref, pc_ref), grad(gx_ref, px_ref)], axis=0)
        parts = [jnp.dot(d, adj_ref[b, k], preferred_element_type=F32) for k in range(slots)]
        for k in range(slots):
            target = jnp.where(k < count_ref[b], cols_ref[k, b] - base, spare)
            acc[target] += parts[k]
    main_ref[...] = acc[reach : reach + blocks]
    before_ref[...] = acc[:reach].astype(BF16)
    after_ref[...] = acc[reach + blocks : spare].astype(BF16)


def link_kernel(
    chunks,
    pick_ref, from_ref, main_ref, before_ref, after_ref, feat_ref, wpiece_ref,
    gw_ref, gf_ref,
    gathered, held, corrupt, outgoing, incoming_first, incoming_second, halo, wall, wpair, total, gw_out, gw_in, gw_sum, gw_last,
    halo_send, halo_recv, w_send, w_recv, un_send, un_recv, cw_send, cw_recv, ccw_send, ccw_recv,
    sib_send, sib_recv, gw_send, gw_recv, last_send, last_recv,
):
    nodes = lax.axis_size("node")
    chans = lax.axis_size("chan")
    n = lax.axis_index("node")
    c = lax.axis_index("chan")
    depth = chans // 2
    half = depth // 2
    z = c // 2
    core = lax.rem(c, 2)
    blocks = main_ref.shape[0]
    width = feat_ref.shape[0]
    rows = main_ref.shape[2]
    reach = before_ref.shape[0]
    part = width // chunks
    incoming = (incoming_first, incoming_second)
    right = 2 * lax.rem(z + 1, depth) + core
    left = 2 * lax.rem(z + depth - 1, depth) + core
    sib = 2 * z + 1 - core
    after = lax.rem(n + 1, nodes)
    before = lax.rem(n + nodes - 1, nodes)
    to_n, to_c = 2 * c + n // chans, lax.rem(n, chans)
    fr_n, fr_c = lax.rem(n, 2) * chans + c, n // 2
    to_self = jnp.logical_and(to_n == n, to_c == c)

    def peer(r):
        return lax.rem(n + r, nodes)

    barrier = pltpu.get_barrier_semaphore()

    @pl.loop(1, nodes)
    def _(r):
        pl.semaphore_signal(barrier, inc=1, device_id=(peer(r), c), device_id_type=MESH)

    for who in (right, left, sib):
        pl.semaphore_signal(barrier, inc=1, device_id=(n, who), device_id_type=MESH)

    @pl.when(jnp.logical_not(to_self))
    def _():
        pl.semaphore_signal(barrier, inc=1, device_id=(fr_n, fr_c), device_id_type=MESH)
        pl.semaphore_wait(barrier, nodes + 3)

    @pl.when(to_self)
    def _():
        pl.semaphore_wait(barrier, nodes + 2)

    def halo_copy(src, slot, to):
        return pltpu.make_async_remote_copy(
            src_ref=src, dst_ref=halo.at[slot], send_sem=halo_send.at[slot], recv_sem=halo_recv.at[slot],
            device_id=(to, c), device_id_type=MESH,
        )

    to_after = halo_copy(after_ref, 0, after)
    to_before = halo_copy(before_ref, 1, before)
    to_after.start()
    to_before.start()

    def w_copy(r, slot):
        return pltpu.make_async_remote_copy(
            src_ref=wpiece_ref, dst_ref=wall.at[slot], send_sem=w_send.at[r], recv_sem=w_recv.at[slot],
            device_id=(peer(r), c), device_id_type=MESH,
        )

    to_after.wait_recv()
    to_before.wait_recv()
    for i in range(blocks):
        block = main_ref[i]
        if i < reach:
            block = block + halo[0, i].astype(F32)
        if i >= blocks - reach:
            block = block + halo[1, i - (blocks - reach)].astype(F32)
        held[i] = block[:width]
        corrupt[i] = block[width:].astype(BF16)

    def un_copy(q, r, dest, slot):
        return pltpu.make_async_remote_copy(
            src_ref=outgoing.at[q, dest], dst_ref=incoming[q].at[slot],
            send_sem=un_send.at[q, r], recv_sem=un_recv.at[q, slot],
            device_id=(dest, c), device_id_type=MESH,
        )

    for q in range(chunks):

        @pl.loop(1, nodes)
        def _(r):
            dest = peer(r)
            outgoing[q, dest] = corrupt[pick_ref[dest], q * part : (q + 1) * part]
            un_copy(q, r, dest, n).start()

        incoming[q][n] = corrupt[pick_ref[n], q * part : (q + 1) * part]

    @pl.loop(1, nodes)
    def _(r):
        w_copy(r, n).start()

    wall[n] = wpiece_ref[...]

    def ring_copy(s, q, to_right):
        shard = 2 * lax.rem(z + (depth - s if to_right else s), depth) + core
        where = gathered.at[shard, pl.ds(q * part, part)]
        return pltpu.make_async_remote_copy(
            src_ref=where, dst_ref=where,
            send_sem=(cw_send if to_right else ccw_send).at[s, q],
            recv_sem=(cw_recv if to_right else ccw_recv).at[s, q],
            device_id=(n, right if to_right else left), device_id_type=MESH,
        )

    def sib_copy(t, zz, q):
        where = gathered.at[2 * zz + core, pl.ds(q * part, part)]
        return pltpu.make_async_remote_copy(
            src_ref=where, dst_ref=where, send_sem=sib_send.at[t, q], recv_sem=sib_recv.at[t, q],
            device_id=(n, sib), device_id_type=MESH,
        )

    def goes(s, q, to_right):
        return s + 1 < half or (s + 1 == half and (q < chunks // 2) == to_right)

    def send_on(s, q, to_right):
        if goes(s, q, to_right):
            ring_copy(s, q, to_right).start()

    for q in range(chunks):

        @pl.loop(1, nodes)
        def _(r):
            un_copy(q, r, peer(r), peer(nodes - r)).wait_recv()

        for i in range(blocks):
            gathered[c, q * part : (q + 1) * part, i * rows : (i + 1) * rows] = (
                held[i, q * part : (q + 1) * part] + incoming[q][from_ref[i]].astype(F32)
            ).astype(BF16)
        send_on(0, q, True)
        send_on(0, q, False)
        sib_copy(0, z, q).start()

    @pl.loop(1, nodes)
    def _(r):
        w_copy(r, peer(nodes - r)).wait_recv()

    low = lax.broadcasted_iota(jnp.int32, wpiece_ref.shape, 1) < width

    def swap(value):
        return pltpu.roll(value, width, 1)

    short = wpiece_ref.shape[0]
    for zz in range(depth):
        for h in range(2):
            one = wall[h * chans + 2 * zz].astype(F32)
            two = wall[h * chans + 2 * zz + 1].astype(F32)
            at = 2 * short * h
            wpair[zz, at : at + short] = jnp.where(low, one, swap(two)).astype(BF16)
            wpair[zz, at + short : at + 2 * short] = jnp.where(low, swap(one), two).astype(BF16)

    total[...] = jnp.zeros_like(total)

    def gw_copy(dest, slot):
        return pltpu.make_async_remote_copy(
            src_ref=gw_out.at[dest], dst_ref=gw_in.at[slot], send_sem=gw_send.at[dest], recv_sem=gw_recv.at[slot],
            device_id=(dest, c), device_id_type=MESH,
        )

    def use(zz):
        pair = gathered[pl.ds(2 * zz, 2)].reshape(2 * width, blocks * rows)
        total[...] += jnp.dot(wpair[zz], pair, preferred_element_type=F32)
        product = lax.dot_general(feat_ref[...], pair, (((1,), (1,)), ((), ())), preferred_element_type=F32)
        for h in range(2):
            top = product[2 * short * h : 2 * short * h + short]
            low_part = product[2 * short * h + short : 2 * short * (h + 1)]
            pieces = (jnp.where(low, top, swap(low_part)), jnp.where(low, swap(top), low_part))
            for k in range(2):
                dest = h * chans + 2 * zz + k
                gw_out[dest] = pieces[k].astype(BF16)

                @pl.when(dest != n)
                def _():
                    gw_copy(dest, n).start()

                @pl.when(dest == n)
                def _():
                    gw_in[n] = pieces[k].astype(BF16)

    def sib_wait(t, zz):
        for q in range(chunks):
            sib_copy(t, zz, q).wait_recv()

    def finish(s):
        if s == 0:
            sib_wait(0, z)
            use(z)
        elif s < half:
            sib_wait(s, z)
            sib_wait(half + s, z)

            @pl.loop(0, 2)
            def _(side):
                use(lax.rem(z + side * s + (1 - side) * (depth - s), depth))
        else:
            sib_wait(half, z)
            use(lax.rem(z + half, depth))

    for s in range(1, half + 1):
        for q in range(chunks):
            if goes(s - 1, q, True):
                ring_copy(s - 1, q, True).wait_recv()
                send_on(s, q, True)
                sib_copy(s, lax.rem(z + depth - s, depth), q).start()
            if goes(s - 1, q, False):
                ring_copy(s - 1, q, False).wait_recv()
                send_on(s, q, False)
                sib_copy(half if s == half else half + s, lax.rem(z + s, depth), q).start()
        finish(s - 1)
    finish(half)
    gf_ref[...] = total[...].astype(BF16)

    @pl.loop(1, nodes)
    def _(r):
        gw_copy(peer(r), peer(nodes - r)).wait_recv()

    gw_sum[...] = jnp.sum(gw_in[...].astype(F32), axis=0)
    last = pltpu.make_async_remote_copy(
        src_ref=gw_sum, dst_ref=gw_last, send_sem=last_send, recv_sem=last_recv,
        device_id=(to_n, to_c), device_id_type=MESH,
    )

    @pl.when(to_self)
    def _():
        gw_ref[...] = gw_sum[...]

    @pl.when(jnp.logical_not(to_self))
    def _():
        last.start()
        last.wait()
        gw_ref[...] = gw_last[...]

    to_after.wait_send()
    to_before.wait_send()

    @pl.loop(1, nodes)
    def _(r):
        w_copy(r, n).wait_send()
        gw_copy(peer(r), n).wait_send()
        for q in range(chunks):
            un_copy(q, r, peer(r), n).wait_send()

    for q in range(chunks):
        for s in range(half):
            for to_right in (True, False):
                if goes(s, q, to_right):
                    ring_copy(s, q, to_right).wait_send()
        for t in range(2 * half):
            sib_copy(t, z, q).wait_send()


def local(
    features, weight, pre_clean, pre_corrupt, grad_clean, grad_corrupt, slopes, adj_vals, adj_cols, adj_count, shuffle_from
):
    nodes, chans = lax.axis_size("node"), lax.axis_size("chan")
    row_count, width = features.shape
    blocks, slots, rows, _ = adj_vals.shape
    reach = (slots - 1) // 2
    half = chans // 4
    chunks = 2
    n = lax.axis_index("node")
    vmem = pl.BlockSpec(memory_space=pltpu.VMEM)
    smem = pl.BlockSpec(memory_space=pltpu.SMEM)

    moved = lax.ppermute(
        weight,
        ("node", "chan"),
        [(a * chans + b, ((a % 2) * chans + b) * chans + a // 2) for a in range(nodes) for b in range(chans)],
    )
    short = weight.shape[0] // 2
    wpiece = jnp.concatenate([moved[:short], moved[short:]], axis=1)

    mine = lax.dynamic_slice_in_dim(shuffle_from, n * blocks, blocks)
    pick = jnp.sum(
        jnp.where((mine // blocks)[:, None] == jnp.arange(nodes)[None, :], jnp.arange(blocks)[:, None], 0), axis=0
    )
    my_blocks = n * blocks + jnp.arange(blocks)
    owner = jnp.arange(shuffle_from.shape[0]) // blocks
    come_from = jnp.sum(jnp.where(shuffle_from[None, :] == my_blocks[:, None], owner[None, :], 0), axis=1)

    slope = jnp.broadcast_to(slopes[:, None], (width, rows))
    main, before, after = pl.pallas_call(
        band_kernel,
        out_shape=(
            jax.ShapeDtypeStruct((blocks, 2 * width, rows), F32),
            jax.ShapeDtypeStruct((reach, 2 * width, rows), BF16),
            jax.ShapeDtypeStruct((reach, 2 * width, rows), BF16),
        ),
        in_specs=[smem, smem] + [vmem] * 6,
        out_specs=(vmem, vmem, vmem),
        scratch_shapes=[pltpu.VMEM((blocks + 2 * reach + 1, 2 * width, rows), F32)],
        compiler_params=pltpu.CompilerParams(vmem_limit_bytes=24 * 2**20),
        cost_estimate=pl.CostEstimate(flops=2 * blocks * slots * rows**3, bytes_accessed=5 * 2**20, transcendentals=0),
        name="band",
    )(adj_cols.T, adj_count, grad_clean.T, pre_clean.T, grad_corrupt.T, pre_corrupt.T, slope, adj_vals)

    part = width // chunks
    dma = pltpu.SemaphoreType.DMA
    gw, gf = pl.pallas_call(
        functools.partial(link_kernel, chunks),
        out_shape=(
            jax.ShapeDtypeStruct((short, 2 * width), F32),
            jax.ShapeDtypeStruct((width, row_count), BF16),
        ),
        in_specs=[smem, smem] + [vmem] * 5,
        out_specs=(vmem, vmem),
        scratch_shapes=[
            pltpu.VMEM((chans, width, row_count), BF16),
            pltpu.VMEM((blocks, width, rows), F32),
            pltpu.VMEM((blocks, width, rows), BF16),
            pltpu.VMEM((chunks, nodes, part, rows), BF16),
            pltpu.VMEM((nodes, part, rows), BF16),
            pltpu.VMEM((nodes, part, rows), BF16),
            pltpu.VMEM((2, reach, 2 * width, rows), BF16),
            pltpu.VMEM((nodes, short, 2 * width), BF16),
            pltpu.VMEM((chans // 2, 4 * short, 2 * width), BF16),
            pltpu.VMEM((width, row_count), F32),
            pltpu.VMEM((nodes, short, 2 * width), BF16),
            pltpu.VMEM((nodes, short, 2 * width), BF16),
            pltpu.VMEM((short, 2 * width), F32),
            pltpu.VMEM((short, 2 * width), F32),
            dma((2,)),
            dma((2,)),
            dma((nodes,)),
            dma((nodes,)),
            dma((chunks, nodes)),
            dma((chunks, nodes)),
            dma((half, chunks)),
            dma((half, chunks)),
            dma((half, chunks)),
            dma((half, chunks)),
            dma((2 * half, chunks)),
            dma((2 * half, chunks)),
            dma((nodes,)),
            dma((nodes,)),
            dma,
            dma,
        ],
        compiler_params=pltpu.CompilerParams(
            collective_id=0, has_side_effects=True, vmem_limit_bytes=32 * 2**20
        ),
        cost_estimate=pl.CostEstimate(
            flops=4 * row_count * width * width * chans, bytes_accessed=8 * 2**20, transcendentals=0
        ),
        name="link",
    )(pick, come_from, main, before, after, features.T, wpiece)
    grad_weight = jnp.concatenate([gw[:, :width], gw[:, width:]], axis=0)
    return (grad_weight, gf.T)


def solution(mesh):
    placed = (
        P("node", "chan"),
        P("node", "chan"),
        P("node", "chan"),
        P("node", "chan"),
        P("node", "chan"),
        P("node", "chan"),
        P("chan"),
        P("node", None, None, None),
        P("node", None),
        P("node"),
        P(),
    )
    return jax.shard_map(
        local,
        mesh=mesh,
        in_specs=placed,
        out_specs=(P("node", "chan"), P("node", "chan")),
        check_vma=False,
    )
```

```python
import functools

import jax
import jax.numpy as jnp
from jax import lax
from jax.experimental import pallas as pl
from jax.experimental.pallas import tpu as pltpu
from jax.sharding import PartitionSpec as P

MESH = pl.DeviceIdType.MESH
BF16 = jnp.bfloat16
F32 = jnp.float32


def band_kernel(
    cols_hbm, count_hbm, shuffle_hbm, gc_hbm, pc_hbm, gx_hbm, px_hbm, slope_hbm, adj_hbm,
    main_ref, before_ref, after_ref, pick_ref, from_ref,
    acc, row_vmem, adj_vmem, cols_ref, count_ref, shuffle_ref, slope_ref, row_sem, adj_sem, small_sem,
):
    blocks, slots, rows, _ = adj_vmem.shape
    nodes = pick_ref.shape[0]
    reach = (slots - 1) // 2
    me = lax.axis_index("node")
    base = me * blocks - reach
    row_copies = [
        pltpu.make_async_copy(hbm, row_vmem.at[i], row_sem.at[i]) for i, hbm in enumerate((gc_hbm, pc_hbm, gx_hbm, px_hbm))
    ]
    adj_copies = [pltpu.make_async_copy(adj_hbm.at[b], adj_vmem.at[b], adj_sem.at[b]) for b in range(blocks)]
    small = ((shuffle_hbm, shuffle_ref), (slope_hbm, slope_ref), (cols_hbm, cols_ref), (count_hbm, count_ref))
    small_copies = [pltpu.make_async_copy(src, dst, small_sem.at[i]) for i, (src, dst) in enumerate(small)]
    for copy in small_copies + row_copies + adj_copies:
        copy.start()
    acc[...] = jnp.zeros_like(acc)
    small_copies[0].wait()

    for d in range(nodes):
        pick_ref[d] = 0
    for i in range(blocks):
        pick_ref[shuffle_ref[me * blocks + i] // blocks] = i

    @pl.loop(0, nodes)
    def _(d):
        for i in range(blocks):
            at = shuffle_ref[d * blocks + i] - me * blocks
            from_ref[jnp.where(jnp.logical_and(at >= 0, at < blocks), at, blocks)] = d

    for copy in small_copies[1:]:
        copy.wait()
    slope = jnp.broadcast_to(slope_ref[...], (rows, slope_ref.shape[1])).T
    spare = blocks + 2 * reach
    for copy in row_copies:
        copy.wait()
    for b in range(blocks):
        here = slice(b * rows, (b + 1) * rows)

        def grad(g, p):
            g = row_vmem[g, :, here].astype(F32)
            return jnp.where(row_vmem[p, :, here].astype(F32) > 0, g, g * slope).astype(BF16)

        d = jnp.concatenate([grad(0, 1), grad(2, 3)], axis=0)
        adj_copies[b].wait()
        parts = [jnp.dot(d, adj_vmem[b, k], preferred_element_type=F32) for k in range(slots)]
        for k in range(slots):
            target = jnp.where(k < count_ref[b], cols_ref[k, b] - base, spare)
            acc[target] += parts[k]
    main_ref[...] = acc[reach : reach + blocks]
    before_ref[...] = acc[:reach].astype(BF16)
    after_ref[...] = acc[reach + blocks : spare].astype(BF16)


def link_kernel(
    chunks,
    pick_hbm, from_hbm, main_hbm, before_hbm, after_hbm, weight_hbm, feat_hbm,
    gw_ref, gf_ref,
    gathered, pick_ref, from_ref, main_ref, corrupt, outgoing, halo, wraw, wown, wgot, wall, wpair, feat, total, gw_out, gw_in, gw_sum, gw_last,
    halo_send, halo_recv, wone_send, wone_recv, w_send, w_recv, un_send, un_recv,
    cw_send, cw_recv, ccw_send, ccw_recv, sib_send, sib_recv, gw_send, gw_recv, last_send, last_recv, feat_sem, in_sem,
    *incoming,
):
    nodes = lax.axis_size("node")
    chans = lax.axis_size("chan")
    n = lax.axis_index("node")
    c = lax.axis_index("chan")
    depth = chans // 2
    half = depth // 2
    z = c // 2
    core = lax.rem(c, 2)
    blocks = main_ref.shape[0]
    width = feat.shape[0]
    rows = main_ref.shape[2]
    reach = before_hbm.shape[0]
    part = width // chunks
    short = wown.shape[0]
    right = 2 * lax.rem(z + 1, depth) + core
    left = 2 * lax.rem(z + depth - 1, depth) + core
    sib = 2 * z + 1 - core
    after = lax.rem(n + 1, nodes)
    before = lax.rem(n + nodes - 1, nodes)
    to_n, to_c = 2 * c + n // chans, lax.rem(n, chans)
    fr_n, fr_c = lax.rem(n, 2) * chans + c, n // 2
    to_self = jnp.logical_and(to_n == n, to_c == c)
    to_other = jnp.logical_not(to_self)

    def peer(r):
        return lax.rem(n + r, nodes)

    feat_copy = pltpu.make_async_copy(feat_hbm, feat, feat_sem)
    moves = ((main_hbm, main_ref), (pick_hbm, pick_ref), (from_hbm, from_ref), (weight_hbm, wraw))
    in_copies = [pltpu.make_async_copy(src, dst, in_sem.at[i]) for i, (src, dst) in enumerate(moves)]
    for copy in in_copies:
        copy.start()
    feat_copy.start()
    barrier = pltpu.get_barrier_semaphore()

    @pl.loop(1, nodes)
    def _(r):
        pl.semaphore_signal(barrier, inc=1, device_id=(peer(r), c), device_id_type=MESH)

    for who in (right, left, sib):
        pl.semaphore_signal(barrier, inc=1, device_id=(n, who), device_id_type=MESH)

    @pl.when(to_other)
    def _():
        pl.semaphore_signal(barrier, inc=1, device_id=(fr_n, fr_c), device_id_type=MESH)
        pl.semaphore_signal(barrier, inc=1, device_id=(to_n, to_c), device_id_type=MESH)

    total[...] = jnp.zeros_like(total)
    for copy in in_copies:
        copy.wait()
    for i in range(reach, blocks - reach):
        corrupt[i] = main_ref[i, width:].astype(BF16)
    wown[...] = jnp.concatenate([wraw[:short].astype(F32), wraw[short:].astype(F32)], axis=1).astype(BF16)

    @pl.when(to_other)
    def _():
        pl.semaphore_wait(barrier, nodes + 4)

    @pl.when(to_self)
    def _():
        pl.semaphore_wait(barrier, nodes + 2)

    def halo_copy(src, slot, side, to):
        return pltpu.make_async_remote_copy(
            src_ref=src.at[:, pl.ds(side * width, width)], dst_ref=halo.at[slot, side],
            send_sem=halo_send.at[slot, side], recv_sem=halo_recv.at[slot, side],
            device_id=(to, c), device_id_type=MESH,
        )

    halos = [[halo_copy(after_hbm, 0, side, after), halo_copy(before_hbm, 1, side, before)] for side in range(2)]
    for side in (1, 0):
        for copy in halos[side]:
            copy.start()

    w_one = pltpu.make_async_remote_copy(
        src_ref=wown, dst_ref=wgot, send_sem=wone_send, recv_sem=wone_recv,
        device_id=(fr_n, fr_c), device_id_type=MESH,
    )

    def w_copy(r, slot):
        return pltpu.make_async_remote_copy(
            src_ref=wgot, dst_ref=wall.at[slot], send_sem=w_send.at[r], recv_sem=w_recv.at[slot],
            device_id=(peer(r), c), device_id_type=MESH,
        )

    @pl.when(to_other)
    def _():
        w_one.start()

    @pl.when(to_self)
    def _():
        wgot[...] = wown[...]

    for copy in halos[1]:
        copy.wait_recv()
    for i in range(reach):
        corrupt[i] = (main_ref[i, width:] + halo[0, 1, i].astype(F32)).astype(BF16)
        j = blocks - reach + i
        corrupt[j] = (main_ref[j, width:] + halo[1, 1, i].astype(F32)).astype(BF16)

    def un_copy(q, r, dest, slot):
        return pltpu.make_async_remote_copy(
            src_ref=outgoing.at[dest, pl.ds(q * part, part)], dst_ref=incoming[q].at[slot],
            send_sem=un_send.at[q, r], recv_sem=un_recv.at[q, slot],
            device_id=(dest, c), device_id_type=MESH,
        )

    @pl.loop(1, nodes)
    def _(r):
        dest = peer(r)
        outgoing[dest] = corrupt[pick_ref[dest]]
        un_copy(0, r, dest, n).start()

    for q in range(1, chunks):

        @pl.loop(1, nodes)
        def _(r):
            un_copy(q, r, peer(r), n).start()

    for q in range(chunks):
        incoming[q][n] = corrupt[pick_ref[n], q * part : (q + 1) * part]

    @pl.when(to_other)
    def _():
        w_one.wait()

    @pl.loop(1, nodes)
    def _(r):
        w_copy(r, n).start()

    wall[n] = wgot[...]
    for copy in halos[0]:
        copy.wait_recv()

    def ring_copy(s, q, to_right):
        shard = 2 * lax.rem(z + (depth - s if to_right else s), depth) + core
        where = gathered.at[shard, pl.ds(q * part, part)]
        return pltpu.make_async_remote_copy(
            src_ref=where, dst_ref=where,
            send_sem=(cw_send if to_right else ccw_send).at[s, q],
            recv_sem=(cw_recv if to_right else ccw_recv).at[s, q],
            device_id=(n, right if to_right else left), device_id_type=MESH,
        )

    def sib_copy(t, zz, q):
        where = gathered.at[2 * zz + core, pl.ds(q * part, part)]
        return pltpu.make_async_remote_copy(
            src_ref=where, dst_ref=where, send_sem=sib_send.at[t, q], recv_sem=sib_recv.at[t, q],
            device_id=(n, sib), device_id_type=MESH,
        )

    def goes(s, q, to_right):
        return s + 1 < half or (s + 1 == half and (q < chunks // 2) == to_right)

    def send_on(s, q, to_right):
        if goes(s, q, to_right):
            ring_copy(s, q, to_right).start()

    def own(q):
        @pl.loop(1, nodes)
        def _(r):
            un_copy(q, r, peer(r), peer(nodes - r)).wait_recv()

        here = slice(q * part, (q + 1) * part)
        for i in range(blocks):
            block = main_ref[i, here] + incoming[q][from_ref[i]].astype(F32)
            if i < reach:
                block = block + halo[0, 0, i, here].astype(F32)
            if i >= blocks - reach:
                block = block + halo[1, 0, i - (blocks - reach), here].astype(F32)
            gathered[c, here, i * rows : (i + 1) * rows] = block.astype(BF16)
        send_on(0, q, True)
        send_on(0, q, False)
        sib_copy(0, z, q).start()

    def step(s, q):
        if goes(s - 1, q, True):
            ring_copy(s - 1, q, True).wait_recv()
            send_on(s, q, True)
            sib_copy(s, lax.rem(z + depth - s, depth), q).start()
        if goes(s - 1, q, False):
            ring_copy(s - 1, q, False).wait_recv()
            send_on(s, q, False)
            sib_copy(half if s == half else half + s, lax.rem(z + s, depth), q).start()

    low = lax.broadcasted_iota(jnp.int32, wown.shape, 1) < width

    def swap(value):
        return pltpu.roll(value, width, 1)

    def weights():
        @pl.loop(1, nodes)
        def _(r):
            w_copy(r, peer(nodes - r)).wait_recv()

        for zz in range(depth):
            for h in range(2):
                one = wall[h * chans + 2 * zz].astype(F32)
                two = wall[h * chans + 2 * zz + 1].astype(F32)
                at = 2 * short * h
                wpair[zz, at : at + short] = jnp.where(low, one, swap(two)).astype(BF16)
                wpair[zz, at + short : at + 2 * short] = jnp.where(low, swap(one), two).astype(BF16)

    def gw_copy(dest, slot):
        return pltpu.make_async_remote_copy(
            src_ref=gw_out.at[dest], dst_ref=gw_in.at[slot], send_sem=gw_send.at[dest], recv_sem=gw_recv.at[slot],
            device_id=(dest, c), device_id_type=MESH,
        )

    def use(zz):
        pair = gathered[pl.ds(2 * zz, 2)].reshape(2 * width, blocks * rows)
        product = lax.dot_general(feat[...], pair, (((1,), (1,)), ((), ())), preferred_element_type=F32)
        for h in range(2):
            top = product[2 * short * h : 2 * short * h + short]
            bottom = product[2 * short * h + short : 2 * short * (h + 1)]
            gw_out[h * chans + 2 * zz] = jnp.where(low, top, swap(bottom)).astype(BF16)
            gw_out[h * chans + 2 * zz + 1] = jnp.where(low, swap(top), bottom).astype(BF16)

    def finish(s):
        sides = (-s, s) if 0 < s < half else (s,)
        for side in sides:
            for q in range(chunks):
                sib_copy(half + s if 0 < side < half else s, z, q).wait_recv()
        count = 4 * len(sides)

        @pl.loop(0, len(sides))
        def _(i):
            use(lax.rem(z + depth - s + 2 * s * i, depth))

        @pl.loop(0, count)
        def _(i):
            j = lax.rem(i + n, count)
            zz = lax.rem(z + depth - s + 2 * s * (j // 4), depth)
            dest = (lax.rem(j, 4) // 2) * chans + 2 * zz + lax.rem(j, 2)

            @pl.when(dest != n)
            def _():
                gw_copy(dest, n).start()

            @pl.when(dest == n)
            def _():
                gw_in[n] = gw_out[n]

        @pl.loop(0, len(sides))
        def _(i):
            zz = lax.rem(z + depth - s + 2 * s * i, depth)
            pair = gathered[pl.ds(2 * zz, 2)].reshape(2 * width, blocks * rows)
            total[...] += jnp.dot(wpair[zz], pair, preferred_element_type=F32)

    for wave in range(half + chunks):
        if wave < chunks:
            own(wave)
        for s in range(half, 0, -1):
            if 0 <= wave - s < chunks:
                step(s, wave - s)
        if wave == chunks - 1:
            feat_copy.wait()
            weights()
        if wave >= chunks:
            finish(wave - chunks)
    finish(half)
    gf_ref[...] = total[...].astype(BF16)

    @pl.loop(1, nodes)
    def _(r):
        gw_copy(peer(r), peer(nodes - r)).wait_recv()

    gw_sum[...] = jnp.sum(gw_in[...].astype(F32), axis=0)
    last = pltpu.make_async_remote_copy(
        src_ref=gw_sum, dst_ref=gw_last, send_sem=last_send, recv_sem=last_recv,
        device_id=(to_n, to_c), device_id_type=MESH,
    )

    @pl.when(to_other)
    def _():
        last.start()

    for side in range(2):
        for copy in halos[side]:
            copy.wait_send()

    @pl.loop(1, nodes)
    def _(r):
        w_copy(r, n).wait_send()
        gw_copy(peer(r), n).wait_send()
        for q in range(chunks):
            un_copy(q, r, peer(r), n).wait_send()

    for q in range(chunks):
        for s in range(half):
            for to_right in (True, False):
                if goes(s, q, to_right):
                    ring_copy(s, q, to_right).wait_send()
        for t in range(2 * half):
            sib_copy(t, z, q).wait_send()

    @pl.when(to_self)
    def _():
        gw_ref[...] = gw_sum[...]

    @pl.when(to_other)
    def _():
        last.wait()
        gw_ref[...] = gw_last[...]


def local(
    features, weight, pre_clean, pre_corrupt, grad_clean, grad_corrupt, slopes, adj_vals, adj_cols, adj_count, shuffle_from
):
    nodes, chans = lax.axis_size("node"), lax.axis_size("chan")
    row_count, width = features.shape
    blocks, slots, rows, _ = adj_vals.shape
    reach = (slots - 1) // 2
    half = chans // 4
    chunks = 4
    short = weight.shape[0] // 2
    part = width // chunks
    vmem = pl.BlockSpec(memory_space=pltpu.VMEM)
    smem = pl.BlockSpec(memory_space=pltpu.SMEM)
    hbm = pl.BlockSpec(memory_space=pltpu.HBM)
    dma = pltpu.SemaphoreType.DMA

    main, before, after, pick, come_from = pl.pallas_call(
        band_kernel,
        out_shape=(
            jax.ShapeDtypeStruct((blocks, 2 * width, rows), F32),
            jax.ShapeDtypeStruct((reach, 2 * width, rows), BF16),
            jax.ShapeDtypeStruct((reach, 2 * width, rows), BF16),
            jax.ShapeDtypeStruct((nodes,), jnp.int32),
            jax.ShapeDtypeStruct((blocks + 2,), jnp.int32),
        ),
        in_specs=[hbm] * 9,
        out_specs=(vmem, vmem, vmem, smem, smem),
        scratch_shapes=[
            pltpu.VMEM((blocks + 2 * reach + 1, 2 * width, rows), F32),
            pltpu.VMEM((4, width, row_count), BF16),
            pltpu.VMEM((blocks, slots, rows, rows), BF16),
            pltpu.SMEM((slots, blocks), jnp.int32),
            pltpu.SMEM((blocks,), jnp.int32),
            pltpu.SMEM((nodes * blocks,), jnp.int32),
            pltpu.VMEM((1, width), F32),
            dma((4,)),
            dma((blocks,)),
            dma((4,)),
        ],
        compiler_params=pltpu.CompilerParams(vmem_limit_bytes=62 * 2**20),
        cost_estimate=pl.CostEstimate(flops=2 * blocks * slots * rows**3, bytes_accessed=5 * 2**20, transcendentals=0),
        name="band",
    )(
        adj_cols.T, adj_count, shuffle_from, grad_clean.T, pre_clean.T, grad_corrupt.T, pre_corrupt.T, slopes[None, :], adj_vals
    )

    gw, gf = pl.pallas_call(
        functools.partial(link_kernel, chunks),
        out_shape=(
            jax.ShapeDtypeStruct((short, 2 * width), F32),
            jax.ShapeDtypeStruct((width, row_count), BF16),
        ),
        in_specs=[hbm] * 7,
        out_specs=(vmem, vmem),
        scratch_shapes=[
            pltpu.VMEM((chans, width, row_count), BF16),
            pltpu.SMEM((nodes,), jnp.int32),
            pltpu.SMEM((blocks + 2,), jnp.int32),
            pltpu.VMEM((blocks, 2 * width, rows), F32),
            pltpu.VMEM((blocks, width, rows), BF16),
            pltpu.VMEM((nodes, width, rows), BF16),
            pltpu.VMEM((2, 2, reach, width, rows), BF16),
            pltpu.VMEM(weight.shape, BF16),
            pltpu.VMEM((short, 2 * width), BF16),
            pltpu.VMEM((short, 2 * width), BF16),
            pltpu.VMEM((nodes, short, 2 * width), BF16),
            pltpu.VMEM((chans // 2, 4 * short, 2 * width), BF16),
            pltpu.VMEM((width, row_count), BF16),
            pltpu.VMEM((width, row_count), F32),
            pltpu.VMEM((nodes, short, 2 * width), BF16),
            pltpu.VMEM((nodes, short, 2 * width), BF16),
            pltpu.VMEM((short, 2 * width), F32),
            pltpu.VMEM((short, 2 * width), F32),
            dma((2, 2)),
            dma((2, 2)),
            dma,
            dma,
            dma((nodes,)),
            dma((nodes,)),
            dma((chunks, nodes)),
            dma((chunks, nodes)),
            dma((half, chunks)),
            dma((half, chunks)),
            dma((half, chunks)),
            dma((half, chunks)),
            dma((2 * half, chunks)),
            dma((2 * half, chunks)),
            dma((nodes,)),
            dma((nodes,)),
            dma,
            dma,
            dma,
            dma((4,)),
        ]
        + [pltpu.VMEM((nodes, part, rows), BF16)] * chunks,
        compiler_params=pltpu.CompilerParams(
            collective_id=0, has_side_effects=True, vmem_limit_bytes=62 * 2**20
        ),
        cost_estimate=pl.CostEstimate(
            flops=4 * row_count * width * width * chans, bytes_accessed=8 * 2**20, transcendentals=0
        ),
        name="link",
    )(pick, come_from, main, before, after, weight, features.T)
    grad_weight = jnp.concatenate([gw[:, :width], gw[:, width:]], axis=0)
    return (grad_weight, gf.T)


def solution(mesh):
    placed = (
        P("node", "chan"),
        P("node", "chan"),
        P("node", "chan"),
        P("node", "chan"),
        P("node", "chan"),
        P("node", "chan"),
        P("chan"),
        P("node", None, None, None),
        P("node", None),
        P("node"),
        P(),
    )
    return jax.shard_map(
        local,
        mesh=mesh,
        in_specs=placed,
        out_specs=(P("node", "chan"), P("node", "chan")),
        check_vma=False,
    )
```

```python
import functools

import jax
import jax.numpy as jnp
from jax import lax
from jax.experimental import pallas as pl
from jax.experimental.pallas import tpu as pltpu
from jax.sharding import PartitionSpec as P

MESH = pl.DeviceIdType.MESH
BF16 = jnp.bfloat16
F32 = jnp.float32


def layer_kernel(
    chunks,
    cols_hbm, count_hbm, shuffle_hbm, gc_hbm, pc_hbm, gx_hbm, px_hbm, slope_hbm, adj_hbm, weight_hbm, feat_hbm,
    gw_ref, gf_ref,
    gathered, pick_ref, from_ref, cols_ref, count_ref, shuffle_ref, slope_ref, row_vmem, adj_vmem, acc,
    edge, corrupt, outgoing, halo, wraw, wown, wgot, wall, wpair, feat, total, gw_out, gw_in, gw_sum, gw_last,
    row_sem, adj_sem, small_sem,
    halo_send, halo_recv, wone_send, wone_recv, w_send, w_recv, un_send, un_recv,
    cw_send, cw_recv, ccw_send, ccw_recv, sib_send, sib_recv, gw_send, gw_recv, last_send, last_recv,
    *incoming,
):
    nodes = lax.axis_size("node")
    chans = lax.axis_size("chan")
    n = lax.axis_index("node")
    c = lax.axis_index("chan")
    depth = chans // 2
    half = depth // 2
    z = c // 2
    core = lax.rem(c, 2)
    blocks, slots, rows, _ = adj_vmem.shape
    width = feat.shape[0]
    reach = (slots - 1) // 2
    part = width // chunks
    short = wown.shape[0]
    right = 2 * lax.rem(z + 1, depth) + core
    left = 2 * lax.rem(z + depth - 1, depth) + core
    sib = 2 * z + 1 - core
    after = lax.rem(n + 1, nodes)
    before = lax.rem(n + nodes - 1, nodes)
    to_n, to_c = 2 * c + n // chans, 2 * lax.rem(n, depth) + lax.rem(n // depth, 2)
    fr_n, fr_c = (2 * lax.rem(n, 2) + core) * depth + z, n // 2
    to_self = jnp.logical_and(to_n == n, to_c == c)
    to_other = jnp.logical_not(to_self)

    def peer(r):
        return lax.rem(n + r, nodes)

    edges = list(range(reach)) + list(range(blocks - reach, blocks))
    order = edges + list(range(reach, blocks - reach))
    row_copies = [
        pltpu.make_async_copy(hbm, row_vmem.at[i], row_sem.at[i]) for i, hbm in enumerate((gc_hbm, pc_hbm, gx_hbm, px_hbm))
    ]
    adj_copies = [pltpu.make_async_copy(adj_hbm.at[b], adj_vmem.at[b], adj_sem.at[b]) for b in range(blocks)]
    small = (
        (cols_hbm, cols_ref), (count_hbm, count_ref), (slope_hbm, slope_ref), (shuffle_hbm, shuffle_ref),
        (weight_hbm, wraw), (feat_hbm, feat),
    )
    small_copies = [pltpu.make_async_copy(src, dst, small_sem.at[i]) for i, (src, dst) in enumerate(small)]
    for copy in small_copies[:3] + row_copies + [adj_copies[b] for b in order] + small_copies[3:]:
        copy.start()

    barrier = pltpu.get_barrier_semaphore()

    @pl.loop(1, nodes)
    def _(r):
        pl.semaphore_signal(barrier, inc=1, device_id=(peer(r), c), device_id_type=MESH)

    for who in (right, left, sib):
        pl.semaphore_signal(barrier, inc=1, device_id=(n, who), device_id_type=MESH)

    @pl.when(to_other)
    def _():
        pl.semaphore_signal(barrier, inc=1, device_id=(fr_n, fr_c), device_id_type=MESH)
        pl.semaphore_signal(barrier, inc=1, device_id=(to_n, to_c), device_id_type=MESH)

    base = n * blocks - reach
    acc[...] = jnp.zeros_like(acc)
    for copy in small_copies[:3]:
        copy.wait()
    slope = jnp.broadcast_to(slope_ref[...], (rows, width)).T
    for copy in row_copies:
        copy.wait()

    def band(b):
        here = slice(b * rows, (b + 1) * rows)

        def grad(g, p):
            g = row_vmem[g, :, here].astype(F32)
            return jnp.where(row_vmem[p, :, here].astype(F32) > 0, g, g * slope).astype(BF16)

        d = jnp.concatenate([grad(0, 1), grad(2, 3)], axis=0)
        adj_copies[b].wait()
        parts = [jnp.dot(d, adj_vmem[b, k], preferred_element_type=F32) for k in range(slots)]
        where = [jnp.where(k < count_ref[b], cols_ref[k, b] - base - b, -1) for k in range(slots)]
        for o in range(slots):
            value = parts[0] if o == reach else None
            for k in range(1, slots):
                term = jnp.where(where[k] == o, parts[k], 0.0)
                value = term if value is None else value + term
            acc[b + o] += value

    for b in edges:
        band(b)
    edge[0] = acc[reach + blocks :].astype(BF16)
    edge[1] = acc[:reach].astype(BF16)
    small_copies[4].wait()
    wown[...] = jnp.concatenate([wraw[:short].astype(F32), wraw[short:].astype(F32)], axis=1).astype(BF16)

    @pl.when(to_other)
    def _():
        pl.semaphore_wait(barrier, nodes + 4)

    @pl.when(to_self)
    def _():
        pl.semaphore_wait(barrier, nodes + 2)

    def halo_copy(slot, side, to):
        return pltpu.make_async_remote_copy(
            src_ref=edge.at[slot, :, pl.ds(side * width, width)], dst_ref=halo.at[slot, side],
            send_sem=halo_send.at[slot, side], recv_sem=halo_recv.at[slot, side],
            device_id=(to, c), device_id_type=MESH,
        )

    halos = [[halo_copy(0, side, after), halo_copy(1, side, before)] for side in range(2)]
    for side in (1, 0):
        for copy in halos[side]:
            copy.start()

    w_one = pltpu.make_async_remote_copy(
        src_ref=wown, dst_ref=wgot, send_sem=wone_send, recv_sem=wone_recv,
        device_id=(fr_n, fr_c), device_id_type=MESH,
    )

    def w_copy(r, slot):
        return pltpu.make_async_remote_copy(
            src_ref=wgot, dst_ref=wall.at[slot], send_sem=w_send.at[r], recv_sem=w_recv.at[slot],
            device_id=(peer(r), c), device_id_type=MESH,
        )

    @pl.when(to_other)
    def _():
        w_one.start()

    @pl.when(to_self)
    def _():
        wgot[...] = wown[...]

    small_copies[3].wait()
    taken = shuffle_ref[...]
    at = lax.broadcasted_iota(jnp.int32, taken.shape, 1)
    scale = (65536 + blocks - 1) // blocks
    taken_node, at_node = (taken * scale) >> 16, (at * scale) >> 16
    mine = at_node == n
    for d in range(nodes):
        pick_ref[d] = jnp.max(jnp.where(jnp.logical_and(mine, taken_node == d), at - n * blocks, 0))
    for i in range(blocks):
        from_ref[i] = jnp.max(jnp.where(taken == n * blocks + i, at_node, 0))

    for b in range(reach, blocks - reach):
        band(b)
    for i in range(reach, blocks - reach):
        corrupt[i] = acc[reach + i, width:].astype(BF16)
    for copy in halos[1]:
        copy.wait_recv()
    for i in range(reach):
        corrupt[i] = (acc[reach + i, width:] + halo[0, 1, i].astype(F32)).astype(BF16)
        j = blocks - reach + i
        corrupt[j] = (acc[reach + j, width:] + halo[1, 1, i].astype(F32)).astype(BF16)

    def un_copy(q, r, dest, slot):
        return pltpu.make_async_remote_copy(
            src_ref=outgoing.at[dest, pl.ds(q * part, part)], dst_ref=incoming[q].at[slot],
            send_sem=un_send.at[q, r], recv_sem=un_recv.at[q, slot],
            device_id=(dest, c), device_id_type=MESH,
        )

    @pl.loop(1, nodes)
    def _(r):
        dest = peer(r)
        outgoing[dest] = corrupt[pick_ref[dest]]
        un_copy(0, r, dest, n).start()

    for q in range(1, chunks):

        @pl.loop(1, nodes)
        def _(r):
            un_copy(q, r, peer(r), n).start()

    for q in range(chunks):
        incoming[q][n] = corrupt[pick_ref[n], q * part : (q + 1) * part]

    @pl.when(to_other)
    def _():
        w_one.wait()

    @pl.loop(1, nodes)
    def _(r):
        w_copy(r, n).start()

    wall[n] = wgot[...]
    for copy in halos[0]:
        copy.wait_recv()

    def ring_copy(s, q, to_right):
        shard = 2 * lax.rem(z + (depth - s if to_right else s), depth) + core
        where = gathered.at[shard, pl.ds(q * part, part)]
        return pltpu.make_async_remote_copy(
            src_ref=where, dst_ref=where,
            send_sem=(cw_send if to_right else ccw_send).at[s, q],
            recv_sem=(cw_recv if to_right else ccw_recv).at[s, q],
            device_id=(n, right if to_right else left), device_id_type=MESH,
        )

    def sib_copy(t, zz, q):
        where = gathered.at[2 * zz + core, pl.ds(q * part, part)]
        return pltpu.make_async_remote_copy(
            src_ref=where, dst_ref=where, send_sem=sib_send.at[t, q], recv_sem=sib_recv.at[t, q],
            device_id=(n, sib), device_id_type=MESH,
        )

    def goes(s, q, to_right):
        return s + 1 < half or (s + 1 == half and (q < chunks // 2) == to_right)

    def send_on(s, q, to_right):
        if goes(s, q, to_right):
            ring_copy(s, q, to_right).start()

    def own(q):
        @pl.loop(1, nodes)
        def _(r):
            un_copy(q, r, peer(r), peer(nodes - r)).wait_recv()

        here = slice(q * part, (q + 1) * part)
        for i in range(blocks):
            block = acc[reach + i, here] + incoming[q][from_ref[i]].astype(F32)
            if i < reach:
                block = block + halo[0, 0, i, here].astype(F32)
            if i >= blocks - reach:
                block = block + halo[1, 0, i - (blocks - reach), here].astype(F32)
            gathered[c, here, i * rows : (i + 1) * rows] = block.astype(BF16)
        send_on(0, q, True)
        send_on(0, q, False)
        sib_copy(0, z, q).start()

    def step(s, q):
        if goes(s - 1, q, True):
            ring_copy(s - 1, q, True).wait_recv()
            send_on(s, q, True)
            sib_copy(s, lax.rem(z + depth - s, depth), q).start()
        if goes(s - 1, q, False):
            ring_copy(s - 1, q, False).wait_recv()
            send_on(s, q, False)
            sib_copy(half if s == half else half + s, lax.rem(z + s, depth), q).start()

    low = lax.broadcasted_iota(jnp.int32, wown.shape, 1) < width

    def swap(value):
        return pltpu.roll(value, width, 1)

    def weights():
        @pl.loop(1, nodes)
        def _(r):
            w_copy(r, peer(nodes - r)).wait_recv()

        for zz in range(depth):
            for h in range(2):
                one = wall[2 * h * depth + zz].astype(F32)
                two = wall[(2 * h + 1) * depth + zz].astype(F32)
                at = 2 * short * h
                wpair[zz, at : at + short] = jnp.where(low, one, swap(two)).astype(BF16)
                wpair[zz, at + short : at + 2 * short] = jnp.where(low, swap(one), two).astype(BF16)

    def gw_copy(dest, slot):
        return pltpu.make_async_remote_copy(
            src_ref=gw_out.at[dest], dst_ref=gw_in.at[slot], send_sem=gw_send.at[dest], recv_sem=gw_recv.at[slot],
            device_id=(dest, c), device_id_type=MESH,
        )

    def use(zz):
        pair = gathered[pl.ds(2 * zz, 2)].reshape(2 * width, blocks * rows)
        product = lax.dot_general(feat[...], pair, (((1,), (1,)), ((), ())), preferred_element_type=F32)
        for h in range(2):
            top = product[2 * short * h : 2 * short * h + short]
            bottom = product[2 * short * h + short : 2 * short * (h + 1)]
            gw_out[2 * h * depth + zz] = jnp.where(low, top, swap(bottom)).astype(BF16)
            gw_out[(2 * h + 1) * depth + zz] = jnp.where(low, swap(top), bottom).astype(BF16)

    def finish(s):
        sides = (-s, s) if 0 < s < half else (s,)
        for side in sides:
            for q in range(chunks):
                sib_copy(half + s if 0 < side < half else s, z, q).wait_recv()
        count = 4 * len(sides)

        @pl.loop(0, len(sides))
        def _(i):
            use(lax.rem(z + depth - s + 2 * s * i, depth))

        @pl.loop(0, count)
        def _(i):
            j = lax.rem(i + n, count)
            zz = lax.rem(z + depth - s + 2 * s * (j // 4), depth)
            dest = lax.rem(j, 4) * depth + zz

            @pl.when(dest != n)
            def _():
                gw_copy(dest, n).start()

            @pl.when(dest == n)
            def _():
                gw_in[n] = gw_out[n]

        @pl.loop(0, len(sides))
        def _(i):
            zz = lax.rem(z + depth - s + 2 * s * i, depth)
            pair = gathered[pl.ds(2 * zz, 2)].reshape(2 * width, blocks * rows)
            value = jnp.dot(wpair[zz], pair, preferred_element_type=F32)
            total[...] = value if s == 0 else total[...] + value

    for q in range(chunks):
        own(q)
    for s in range(1, half + 1):
        for q in range(chunks):
            step(s, q)
        if s == 1:
            small_copies[5].wait()
            weights()
        finish(s - 1)
    finish(half)
    gf_ref[...] = total[...].astype(BF16)

    @pl.loop(1, nodes)
    def _(r):
        gw_copy(peer(r), peer(nodes - r)).wait_recv()

    gw_sum[...] = jnp.sum(gw_in[...].astype(F32), axis=0)
    last = pltpu.make_async_remote_copy(
        src_ref=gw_sum, dst_ref=gw_last, send_sem=last_send, recv_sem=last_recv,
        device_id=(to_n, to_c), device_id_type=MESH,
    )

    @pl.when(to_other)
    def _():
        last.start()

    for side in range(2):
        for copy in halos[side]:
            copy.wait_send()

    @pl.loop(1, nodes)
    def _(r):
        w_copy(r, n).wait_send()
        gw_copy(peer(r), n).wait_send()
        for q in range(chunks):
            un_copy(q, r, peer(r), n).wait_send()

    for q in range(chunks):
        for s in range(half):
            for to_right in (True, False):
                if goes(s, q, to_right):
                    ring_copy(s, q, to_right).wait_send()
        for t in range(2 * half):
            sib_copy(t, z, q).wait_send()

    @pl.when(to_self)
    def _():
        gw_last[...] = gw_sum[...]

    @pl.when(to_other)
    def _():
        last.wait()

    gw_ref[:short] = gw_last[:, :width]
    gw_ref[short:] = swap(gw_last[...])[:, :width]


def local(
    features, weight, pre_clean, pre_corrupt, grad_clean, grad_corrupt, slopes, adj_vals, adj_cols, adj_count, shuffle_from
):
    nodes, chans = lax.axis_size("node"), lax.axis_size("chan")
    row_count, width = features.shape
    blocks, slots, rows, _ = adj_vals.shape
    reach = (slots - 1) // 2
    half = chans // 4
    chunks = 2
    short = weight.shape[0] // 2
    part = width // chunks
    vmem = pl.BlockSpec(memory_space=pltpu.VMEM)
    hbm = pl.BlockSpec(memory_space=pltpu.HBM)
    dma = pltpu.SemaphoreType.DMA
    gw, gf = pl.pallas_call(
        functools.partial(layer_kernel, chunks),
        out_shape=(
            jax.ShapeDtypeStruct((2 * short, width), F32),
            jax.ShapeDtypeStruct((width, row_count), BF16),
        ),
        in_specs=[hbm] * 11,
        out_specs=(vmem, vmem),
        scratch_shapes=[
            pltpu.VMEM((chans, width, row_count), BF16),
            pltpu.SMEM((nodes,), jnp.int32),
            pltpu.SMEM((blocks,), jnp.int32),
            pltpu.SMEM((slots, blocks), jnp.int32),
            pltpu.SMEM((blocks,), jnp.int32),
            pltpu.VMEM((1, nodes * blocks), jnp.int32),
            pltpu.VMEM((1, width), F32),
            pltpu.VMEM((4, width, row_count), BF16),
            pltpu.VMEM((blocks, slots, rows, rows), BF16),
            pltpu.VMEM((blocks + 2 * reach, 2 * width, rows), F32),
            pltpu.VMEM((2, reach, 2 * width, rows), BF16),
            pltpu.VMEM((blocks, width, rows), BF16),
            pltpu.VMEM((nodes, width, rows), BF16),
            pltpu.VMEM((2, 2, reach, width, rows), BF16),
            pltpu.VMEM(weight.shape, BF16),
            pltpu.VMEM((short, 2 * width), BF16),
            pltpu.VMEM((short, 2 * width), BF16),
            pltpu.VMEM((nodes, short, 2 * width), BF16),
            pltpu.VMEM((chans // 2, 4 * short, 2 * width), BF16),
            pltpu.VMEM((width, row_count), BF16),
            pltpu.VMEM((width, row_count), F32),
            pltpu.VMEM((nodes, short, 2 * width), BF16),
            pltpu.VMEM((nodes, short, 2 * width), BF16),
            pltpu.VMEM((short, 2 * width), F32),
            pltpu.VMEM((short, 2 * width), F32),
            dma((4,)),
            dma((blocks,)),
            dma((6,)),
            dma((2, 2)),
            dma((2, 2)),
            dma,
            dma,
            dma((nodes,)),
            dma((nodes,)),
            dma((chunks, nodes)),
            dma((chunks, nodes)),
            dma((half, chunks)),
            dma((half, chunks)),
            dma((half, chunks)),
            dma((half, chunks)),
            dma((2 * half, chunks)),
            dma((2 * half, chunks)),
            dma((nodes,)),
            dma((nodes,)),
            dma,
            dma,
        ]
        + [pltpu.VMEM((nodes, part, rows), BF16)] * chunks,
        compiler_params=pltpu.CompilerParams(
            collective_id=0, has_side_effects=True, vmem_limit_bytes=62 * 2**20
        ),
        cost_estimate=pl.CostEstimate(
            flops=4 * row_count * width * width * chans, bytes_accessed=8 * 2**20, transcendentals=0
        ),
        name="layer",
    )(
        adj_cols.T, adj_count, shuffle_from[None, :], grad_clean.T, pre_clean.T, grad_corrupt.T, pre_corrupt.T,
        slopes[None, :], adj_vals, weight, features.T,
    )
    return (gw, gf.T)


def solution(mesh):
    placed = (
        P("node", "chan"),
        P("node", "chan"),
        P("node", "chan"),
        P("node", "chan"),
        P("node", "chan"),
        P("node", "chan"),
        P("chan"),
        P("node", None, None, None),
        P("node", None),
        P("node"),
        P(),
    )
    return jax.shard_map(
        local,
        mesh=mesh,
        in_specs=placed,
        out_specs=(P("node", "chan"), P("node", "chan")),
        check_vma=False,
    )
```

```python
import functools

import jax
import jax.numpy as jnp
from jax import lax
from jax.experimental import pallas as pl
from jax.experimental.pallas import tpu as pltpu
from jax.sharding import PartitionSpec as P

MESH = pl.DeviceIdType.MESH
BF16 = jnp.bfloat16
F32 = jnp.float32


def layer_kernel(
    chunks,
    cols_hbm, count_hbm, shuffle_hbm, gc_hbm, pc_hbm, gx_hbm, px_hbm, slope_hbm, adj_hbm, weight_hbm, feat_hbm,
    gw_ref, gf_hbm,
    gathered, gf_ref, pick_ref, from_ref, cols_ref, count_ref, shuffle_ref, slope_ref, row_vmem, adj_vmem, acc,
    edge, corrupt, outgoing, halo, wraw, wown, wgot, wall, wrows, feat, gw_out, gw_in, gw_sum, gw_last,
    row_sem, adj_sem, small_sem,
    halo_send, halo_recv, wone_send, wone_recv, w_send, w_recv, un_send, un_recv,
    cw_send, cw_recv, ccw_send, ccw_recv, sib_send, sib_recv, gw_send, gw_recv, last_send, last_recv, gf_sem,
    *incoming,
):
    nodes = lax.axis_size("node")
    chans = lax.axis_size("chan")
    n = lax.axis_index("node")
    c = lax.axis_index("chan")
    depth = chans // 2
    half = depth // 2
    z = c // 2
    core = lax.rem(c, 2)
    blocks, slots, rows, _ = adj_vmem.shape
    width = feat.shape[0]
    reach = (slots - 1) // 2
    part = width // chunks
    short = wown.shape[0]
    right = 2 * lax.rem(z + 1, depth) + core
    left = 2 * lax.rem(z + depth - 1, depth) + core
    sib = 2 * z + 1 - core
    after = lax.rem(n + 1, nodes)
    before = lax.rem(n + nodes - 1, nodes)
    to_n, to_c = 2 * c + n // chans, 2 * lax.rem(n, depth) + lax.rem(n // depth, 2)
    fr_n, fr_c = (2 * lax.rem(n, 2) + core) * depth + z, n // 2
    to_self = jnp.logical_and(to_n == n, to_c == c)
    to_other = jnp.logical_not(to_self)

    def peer(r):
        return lax.rem(n + r, nodes)

    def turn(r):
        return lax.rem(n + jnp.where(lax.rem(r, 2) == 1, (r + 1) // 2, nodes - r // 2), nodes)

    edges = list(range(reach)) + list(range(blocks - reach, blocks))
    order = edges + list(range(reach, blocks - reach))
    row_copies = [
        pltpu.make_async_copy(hbm, row_vmem.at[i], row_sem.at[i]) for i, hbm in enumerate((gc_hbm, pc_hbm, gx_hbm, px_hbm))
    ]
    adj_copies = [pltpu.make_async_copy(adj_hbm.at[b], adj_vmem.at[b], adj_sem.at[b]) for b in range(blocks)]
    small = (
        (cols_hbm, cols_ref), (count_hbm, count_ref), (slope_hbm, slope_ref), (shuffle_hbm, shuffle_ref),
        (weight_hbm, wraw), (feat_hbm, feat),
    )
    small_copies = [pltpu.make_async_copy(src, dst, small_sem.at[i]) for i, (src, dst) in enumerate(small)]
    for copy in small_copies[:3] + row_copies + [adj_copies[b] for b in order] + small_copies[3:]:
        copy.start()

    barrier = pltpu.get_barrier_semaphore()

    @pl.loop(1, nodes)
    def _(r):
        pl.semaphore_signal(barrier, inc=1, device_id=(peer(r), c), device_id_type=MESH)

    for who in (right, left, sib):
        pl.semaphore_signal(barrier, inc=1, device_id=(n, who), device_id_type=MESH)

    @pl.when(to_other)
    def _():
        pl.semaphore_signal(barrier, inc=1, device_id=(fr_n, fr_c), device_id_type=MESH)
        pl.semaphore_signal(barrier, inc=1, device_id=(to_n, to_c), device_id_type=MESH)

    base = n * blocks - reach
    acc[...] = jnp.zeros_like(acc)
    for copy in small_copies[:3]:
        copy.wait()
    slope = jnp.broadcast_to(slope_ref[...], (rows, width)).T
    for copy in row_copies:
        copy.wait()

    def band(b):
        here = slice(b * rows, (b + 1) * rows)

        def grad(g, p):
            g = row_vmem[g, :, here].astype(F32)
            return jnp.where(row_vmem[p, :, here].astype(F32) > 0, g, g * slope).astype(BF16)

        d = jnp.concatenate([grad(0, 1), grad(2, 3)], axis=0)
        adj_copies[b].wait()
        parts = [jnp.dot(d, adj_vmem[b, k], preferred_element_type=F32) for k in range(slots)]
        where = [jnp.where(k < count_ref[b], cols_ref[k, b] - base - b, -1) for k in range(slots)]
        for o in range(slots):
            value = parts[0] if o == reach else None
            for k in range(1, slots):
                term = jnp.where(where[k] == o, parts[k], 0.0)
                value = term if value is None else value + term
            acc[b + o] += value

    for b in edges:
        band(b)
    edge[0] = acc[reach + blocks :].astype(BF16)
    edge[1] = acc[:reach].astype(BF16)
    small_copies[4].wait()
    wown[...] = jnp.concatenate([wraw[:short].astype(F32), wraw[short:].astype(F32)], axis=1).astype(BF16)

    @pl.when(to_other)
    def _():
        pl.semaphore_wait(barrier, nodes + 4)

    @pl.when(to_self)
    def _():
        pl.semaphore_wait(barrier, nodes + 2)

    def halo_copy(slot, side, to):
        return pltpu.make_async_remote_copy(
            src_ref=edge.at[slot, :, pl.ds(side * width, width)], dst_ref=halo.at[slot, side],
            send_sem=halo_send.at[slot, side], recv_sem=halo_recv.at[slot, side],
            device_id=(to, c), device_id_type=MESH,
        )

    halos = [[halo_copy(0, side, after), halo_copy(1, side, before)] for side in range(2)]
    for side in (1, 0):
        for copy in halos[side]:
            copy.start()

    w_one = pltpu.make_async_remote_copy(
        src_ref=wown, dst_ref=wgot, send_sem=wone_send, recv_sem=wone_recv,
        device_id=(fr_n, fr_c), device_id_type=MESH,
    )

    def w_copy(r, slot):
        return pltpu.make_async_remote_copy(
            src_ref=wgot, dst_ref=wall.at[slot], send_sem=w_send.at[r], recv_sem=w_recv.at[slot],
            device_id=(turn(r), c), device_id_type=MESH,
        )

    @pl.when(to_other)
    def _():
        w_one.start()

    @pl.when(to_self)
    def _():
        wgot[...] = wown[...]

    small_copies[3].wait()
    taken = shuffle_ref[...]
    at = lax.broadcasted_iota(jnp.int32, taken.shape, 1)
    scale = (65536 + blocks - 1) // blocks
    taken_node, at_node = (taken * scale) >> 16, (at * scale) >> 16
    mine = at_node == n
    for d in range(nodes):
        pick_ref[d] = jnp.max(jnp.where(jnp.logical_and(mine, taken_node == d), at - n * blocks, 0))
    for i in range(blocks):
        from_ref[i] = jnp.max(jnp.where(taken == n * blocks + i, at_node, 0))

    for b in range(reach, blocks - reach):
        band(b)
    for i in range(reach, blocks - reach):
        corrupt[i] = acc[reach + i, width:].astype(BF16)
    for copy in halos[1]:
        copy.wait_recv()
    for i in range(reach):
        corrupt[i] = (acc[reach + i, width:] + halo[0, 1, i].astype(F32)).astype(BF16)
        j = blocks - reach + i
        corrupt[j] = (acc[reach + j, width:] + halo[1, 1, i].astype(F32)).astype(BF16)

    def un_copy(q, r, dest, slot):
        return pltpu.make_async_remote_copy(
            src_ref=outgoing.at[dest, pl.ds(q * part, part)], dst_ref=incoming[q].at[slot],
            send_sem=un_send.at[q, r], recv_sem=un_recv.at[q, slot],
            device_id=(dest, c), device_id_type=MESH,
        )

    @pl.loop(1, nodes)
    def _(r):
        dest = turn(r)
        outgoing[dest] = corrupt[pick_ref[dest]]
        un_copy(0, r, dest, n).start()

    for q in range(1, chunks):

        @pl.loop(1, nodes)
        def _(r):
            un_copy(q, r, turn(r), n).start()

    for q in range(chunks):
        incoming[q][n] = corrupt[pick_ref[n], q * part : (q + 1) * part]

    for copy in halos[0]:
        copy.wait_recv()

    def ring_copy(s, q, to_right):
        shard = 2 * lax.rem(z + (depth - s if to_right else s), depth) + core
        where = gathered.at[shard, pl.ds(q * part, part)]
        return pltpu.make_async_remote_copy(
            src_ref=where, dst_ref=where,
            send_sem=(cw_send if to_right else ccw_send).at[s, q],
            recv_sem=(cw_recv if to_right else ccw_recv).at[s, q],
            device_id=(n, right if to_right else left), device_id_type=MESH,
        )

    def sib_copy(t, zz, q):
        where = gathered.at[2 * zz + core, pl.ds(q * part, part)]
        return pltpu.make_async_remote_copy(
            src_ref=where, dst_ref=where, send_sem=sib_send.at[t, q], recv_sem=sib_recv.at[t, q],
            device_id=(n, sib), device_id_type=MESH,
        )

    def goes(s, q, to_right):
        return s + 1 < half or (s + 1 == half and (q < chunks // 2) == to_right)

    def send_on(s, q, to_right):
        if goes(s, q, to_right):
            ring_copy(s, q, to_right).start()

    def own(q):
        @pl.loop(1, nodes)
        def _(r):
            un_copy(q, r, peer(r), peer(nodes - r)).wait_recv()

        here = slice(q * part, (q + 1) * part)
        for i in range(blocks):
            block = acc[reach + i, here] + incoming[q][from_ref[i]].astype(F32)
            if i < reach:
                block = block + halo[0, 0, i, here].astype(F32)
            if i >= blocks - reach:
                block = block + halo[1, 0, i - (blocks - reach), here].astype(F32)
            gathered[c, here, i * rows : (i + 1) * rows] = block.astype(BF16)
        send_on(0, q, True)
        send_on(0, q, False)
        sib_copy(0, z, q).start()

    def step(s, q):
        if goes(s - 1, q, True):
            ring_copy(s - 1, q, True).wait_recv()
            send_on(s, q, True)
            sib_copy(s, lax.rem(z + depth - s, depth), q).start()
        if goes(s - 1, q, False):
            ring_copy(s - 1, q, False).wait_recv()
            send_on(s, q, False)
            sib_copy(half if s == half else half + s, lax.rem(z + s, depth), q).start()

    low = lax.broadcasted_iota(jnp.int32, wown.shape, 1) < width

    def swap(value):
        return pltpu.roll(value, width, 1)

    def weights():
        @pl.loop(1, nodes)
        def _(r):
            w_copy(r, peer(nodes - r)).wait_recv()

        for zz in range(depth):
            here = slice(2 * width * zz, 2 * width * (zz + 1))
            for h in range(2):
                one = wall[2 * h * depth + zz].astype(F32)
                two = wall[(2 * h + 1) * depth + zz].astype(F32)
                at = 2 * short * h
                wrows[at : at + short, here] = jnp.where(low, one, swap(two)).astype(BF16)
                wrows[at + short : at + 2 * short, here] = jnp.where(low, swap(one), two).astype(BF16)

    def gw_copy(dest, slot):
        return pltpu.make_async_remote_copy(
            src_ref=gw_out.at[dest], dst_ref=gw_in.at[slot], send_sem=gw_send.at[dest], recv_sem=gw_recv.at[slot],
            device_id=(dest, c), device_id_type=MESH,
        )

    def use(zz):
        pair = gathered[pl.ds(2 * zz, 2)].reshape(2 * width, blocks * rows)
        product = lax.dot_general(feat[...], pair, (((1,), (1,)), ((), ())), preferred_element_type=F32)
        for h in range(2):
            top = product[2 * short * h : 2 * short * h + short]
            bottom = product[2 * short * h + short : 2 * short * (h + 1)]
            gw_out[2 * h * depth + zz] = jnp.where(low, top, swap(bottom)).astype(BF16)
            gw_out[(2 * h + 1) * depth + zz] = jnp.where(low, swap(top), bottom).astype(BF16)

    def finish(s):
        sides = (-s, s) if 0 < s < half else (s,)
        for side in sides:
            for q in range(chunks):
                sib_copy(half + s if 0 < side < half else s, z, q).wait_recv()
        count = 4 * len(sides)

        @pl.loop(0, len(sides))
        def _(i):
            use(lax.rem(z + depth - s + 2 * s * i, depth))

        @pl.loop(0, count)
        def _(i):
            j = lax.rem(i + n, count)
            zz = lax.rem(z + depth - s + 2 * s * (j // 4), depth)
            dest = lax.rem(j, 4) * depth + zz

            @pl.when(dest != n)
            def _():
                gw_copy(dest, n).start()

            @pl.when(dest == n)
            def _():
                gw_in[n] = gw_out[n]

    for q in range(chunks):
        own(q)
    for s in range(1, half + 1):
        for q in range(chunks):
            step(s, q)
        if s == 1:
            small_copies[5].wait()

            @pl.when(to_other)
            def _():
                w_one.wait()

            wall[n] = wgot[...]
        if s < half:

            @pl.loop(1 + (nodes - 1) * (s - 1) // (half - 1), 1 + (nodes - 1) * s // (half - 1))
            def _(r):
                w_copy(r, n).start()

        finish(s - 1)
    if half == 1:

        @pl.loop(1, nodes)
        def _(r):
            w_copy(r, n).start()

    finish(half)
    weights()
    tile = 2 * rows
    for at in range(0, blocks * rows, tile):
        sums = gathered[:, :, at : at + tile].reshape(chans * width, tile)
        gf_ref[:, at : at + tile] = jnp.dot(wrows[...], sums, preferred_element_type=F32).astype(BF16)
    gf_copy = pltpu.make_async_copy(gf_ref, gf_hbm, gf_sem)
    gf_copy.start()

    @pl.loop(1, nodes)
    def _(r):
        gw_copy(peer(r), peer(nodes - r)).wait_recv()

    gw_sum[...] = jnp.sum(gw_in[...].astype(F32), axis=0)
    last = pltpu.make_async_remote_copy(
        src_ref=gw_sum, dst_ref=gw_last, send_sem=last_send, recv_sem=last_recv,
        device_id=(to_n, to_c), device_id_type=MESH,
    )

    @pl.when(to_other)
    def _():
        last.start()

    for side in range(2):
        for copy in halos[side]:
            copy.wait_send()

    @pl.loop(1, nodes)
    def _(r):
        w_copy(r, n).wait_send()
        gw_copy(peer(r), n).wait_send()
        for q in range(chunks):
            un_copy(q, r, peer(r), n).wait_send()

    for q in range(chunks):
        for s in range(half):
            for to_right in (True, False):
                if goes(s, q, to_right):
                    ring_copy(s, q, to_right).wait_send()
        for t in range(2 * half):
            sib_copy(t, z, q).wait_send()

    @pl.when(to_self)
    def _():
        gw_last[...] = gw_sum[...]

    @pl.when(to_other)
    def _():
        last.wait()

    piece = gw_last[...]
    gw_ref[:short] = piece[:, :width]
    gw_ref[short:] = swap(piece)[:, :width]
    gf_copy.wait()


def local(
    features, weight, pre_clean, pre_corrupt, grad_clean, grad_corrupt, slopes, adj_vals, adj_cols, adj_count, shuffle_from
):
    nodes, chans = lax.axis_size("node"), lax.axis_size("chan")
    row_count, width = features.shape
    blocks, slots, rows, _ = adj_vals.shape
    reach = (slots - 1) // 2
    half = chans // 4
    chunks = 2
    short = weight.shape[0] // 2
    part = width // chunks
    vmem = pl.BlockSpec(memory_space=pltpu.VMEM)
    hbm = pl.BlockSpec(memory_space=pltpu.HBM)
    dma = pltpu.SemaphoreType.DMA
    gw, gf = pl.pallas_call(
        functools.partial(layer_kernel, chunks),
        out_shape=(
            jax.ShapeDtypeStruct((2 * short, width), F32),
            jax.ShapeDtypeStruct((width, row_count), BF16),
        ),
        in_specs=[hbm] * 11,
        out_specs=(vmem, hbm),
        scratch_shapes=[
            pltpu.VMEM((chans, width, row_count), BF16),
            pltpu.VMEM((width, row_count), BF16),
            pltpu.SMEM((nodes,), jnp.int32),
            pltpu.SMEM((blocks,), jnp.int32),
            pltpu.SMEM((slots, blocks), jnp.int32),
            pltpu.SMEM((blocks,), jnp.int32),
            pltpu.VMEM((1, nodes * blocks), jnp.int32),
            pltpu.VMEM((1, width), F32),
            pltpu.VMEM((4, width, row_count), BF16),
            pltpu.VMEM((blocks, slots, rows, rows), BF16),
            pltpu.VMEM((blocks + 2 * reach, 2 * width, rows), F32),
            pltpu.VMEM((2, reach, 2 * width, rows), BF16),
            pltpu.VMEM((blocks, width, rows), BF16),
            pltpu.VMEM((nodes, width, rows), BF16),
            pltpu.VMEM((2, 2, reach, width, rows), BF16),
            pltpu.VMEM(weight.shape, BF16),
            pltpu.VMEM((short, 2 * width), BF16),
            pltpu.VMEM((short, 2 * width), BF16),
            pltpu.VMEM((nodes, short, 2 * width), BF16),
            pltpu.VMEM((4 * short, chans * width), BF16),
            pltpu.VMEM((width, row_count), BF16),
            pltpu.VMEM((nodes, short, 2 * width), BF16),
            pltpu.VMEM((nodes, short, 2 * width), BF16),
            pltpu.VMEM((short, 2 * width), F32),
            pltpu.VMEM((short, 2 * width), F32),
            dma((4,)),
            dma((blocks,)),
            dma((6,)),
            dma((2, 2)),
            dma((2, 2)),
            dma,
            dma,
            dma((nodes,)),
            dma((nodes,)),
            dma((chunks, nodes)),
            dma((chunks, nodes)),
            dma((half, chunks)),
            dma((half, chunks)),
            dma((half, chunks)),
            dma((half, chunks)),
            dma((2 * half, chunks)),
            dma((2 * half, chunks)),
            dma((nodes,)),
            dma((nodes,)),
            dma,
            dma,
            dma,
        ]
        + [pltpu.VMEM((nodes, part, rows), BF16)] * chunks,
        compiler_params=pltpu.CompilerParams(
            collective_id=0, has_side_effects=True, vmem_limit_bytes=62 * 2**20
        ),
        cost_estimate=pl.CostEstimate(
            flops=4 * row_count * width * width * chans, bytes_accessed=8 * 2**20, transcendentals=0
        ),
        name="layer",
    )(
        adj_cols.T, adj_count, shuffle_from[None, :], grad_clean.T, pre_clean.T, grad_corrupt.T, pre_corrupt.T,
        slopes[None, :], adj_vals, weight, features.T,
    )
    return (gw, gf.T)


def solution(mesh):
    placed = (
        P("node", "chan"),
        P("node", "chan"),
        P("node", "chan"),
        P("node", "chan"),
        P("node", "chan"),
        P("node", "chan"),
        P("chan"),
        P("node", None, None, None),
        P("node", None),
        P("node"),
        P(),
    )
    return jax.shard_map(
        local,
        mesh=mesh,
        in_specs=placed,
        out_specs=(P("node", "chan"), P("node", "chan")),
        check_vma=False,
    )
```

```python
import functools

import jax
import jax.numpy as jnp
from jax import lax
from jax.experimental import pallas as pl
from jax.experimental.pallas import tpu as pltpu
from jax.sharding import PartitionSpec as P

MESH = pl.DeviceIdType.MESH
BF16 = jnp.bfloat16
F32 = jnp.float32


def layer_kernel(
    chunks,
    cols_hbm, count_hbm, shuffle_hbm, gc_hbm, pc_hbm, gx_hbm, px_hbm, slope_hbm, adj_hbm, weight_hbm, feat_hbm,
    gw_ref, gf_hbm,
    gathered, gf_ref, pick_ref, from_ref, cols_ref, count_ref, shuffle_ref, slope_ref, row_vmem, adj_vmem, acc,
    edge, corrupt, outgoing, halo, wraw, wown, wgot, wall, wrows, feat, gw_out, gw_in, gw_sum, gw_last,
    row_sem, adj_sem, small_sem,
    halo_send, halo_recv, wone_send, wone_recv, w_send, w_recv, un_send, un_recv,
    cw_send, cw_recv, ccw_send, ccw_recv, sib_send, sib_recv, gw_send, gw_recv, last_send, last_recv, gf_sem,
    *incoming,
):
    nodes = lax.axis_size("node")
    chans = lax.axis_size("chan")
    n = lax.axis_index("node")
    c = lax.axis_index("chan")
    depth = chans // 2
    half = depth // 2
    z = c // 2
    core = lax.rem(c, 2)
    blocks, slots, rows, _ = adj_vmem.shape
    width = feat.shape[0]
    reach = (slots - 1) // 2
    part = width // chunks
    short = wown.shape[0]
    right = 2 * lax.rem(z + 1, depth) + core
    left = 2 * lax.rem(z + depth - 1, depth) + core
    sib = 2 * z + 1 - core
    after = lax.rem(n + 1, nodes)
    before = lax.rem(n + nodes - 1, nodes)
    to_n, to_c = 2 * c + n // chans, 2 * lax.rem(n, depth) + lax.rem(n // depth, 2)
    fr_n, fr_c = (2 * lax.rem(n, 2) + core) * depth + z, n // 2
    to_self = jnp.logical_and(to_n == n, to_c == c)
    to_other = jnp.logical_not(to_self)

    def peer(r):
        return lax.rem(n + r, nodes)

    def turn(r):
        return lax.rem(n + jnp.where(lax.rem(r, 2) == 1, (r + 1) // 2, nodes - r // 2), nodes)

    edges = list(range(reach)) + list(range(blocks - reach, blocks))
    order = edges + list(range(reach, blocks - reach))
    row_copies = [
        pltpu.make_async_copy(hbm, row_vmem.at[i], row_sem.at[i]) for i, hbm in enumerate((gc_hbm, pc_hbm, gx_hbm, px_hbm))
    ]
    adj_copies = [pltpu.make_async_copy(adj_hbm.at[b], adj_vmem.at[b], adj_sem.at[b]) for b in range(blocks)]
    small = (
        (cols_hbm, cols_ref), (count_hbm, count_ref), (slope_hbm, slope_ref), (shuffle_hbm, shuffle_ref),
        (weight_hbm, wraw), (feat_hbm, feat),
    )
    small_copies = [pltpu.make_async_copy(src, dst, small_sem.at[i]) for i, (src, dst) in enumerate(small)]
    for copy in small_copies[:3] + row_copies + [adj_copies[b] for b in order] + small_copies[3:]:
        copy.start()

    barrier = pltpu.get_barrier_semaphore()

    @pl.loop(1, nodes)
    def _(r):
        pl.semaphore_signal(barrier, inc=1, device_id=(peer(r), c), device_id_type=MESH)

    for who in (right, left, sib):
        pl.semaphore_signal(barrier, inc=1, device_id=(n, who), device_id_type=MESH)

    @pl.when(to_other)
    def _():
        pl.semaphore_signal(barrier, inc=1, device_id=(fr_n, fr_c), device_id_type=MESH)
        pl.semaphore_signal(barrier, inc=1, device_id=(to_n, to_c), device_id_type=MESH)

    base = n * blocks - reach
    acc[...] = jnp.zeros_like(acc)
    for copy in small_copies[:3]:
        copy.wait()
    slope = jnp.broadcast_to(slope_ref[...], (rows, width)).T
    for copy in row_copies:
        copy.wait()

    def band(b):
        here = slice(b * rows, (b + 1) * rows)

        def grad(g, p):
            g = row_vmem[g, :, here].astype(F32)
            return jnp.where(row_vmem[p, :, here].astype(F32) > 0, g, g * slope).astype(BF16)

        d = jnp.concatenate([grad(0, 1), grad(2, 3)], axis=0)
        adj_copies[b].wait()
        parts = [jnp.dot(d, adj_vmem[b, k], preferred_element_type=F32) for k in range(slots)]
        where = [jnp.where(k < count_ref[b], cols_ref[k, b] - base - b, -1) for k in range(slots)]
        for o in range(slots):
            value = parts[0] if o == reach else None
            for k in range(1, slots):
                term = jnp.where(where[k] == o, parts[k], 0.0)
                value = term if value is None else value + term
            acc[b + o] += value

    for b in edges:
        band(b)
    edge[0] = acc[reach + blocks :].astype(BF16)
    edge[1] = acc[:reach].astype(BF16)
    small_copies[4].wait()
    wown[...] = jnp.concatenate([wraw[:short].astype(F32), wraw[short:].astype(F32)], axis=1).astype(BF16)

    @pl.when(to_other)
    def _():
        pl.semaphore_wait(barrier, nodes + 4)

    @pl.when(to_self)
    def _():
        pl.semaphore_wait(barrier, nodes + 2)

    def halo_copy(slot, side, to):
        return pltpu.make_async_remote_copy(
            src_ref=edge.at[slot, :, pl.ds(side * width, width)], dst_ref=halo.at[slot, side],
            send_sem=halo_send.at[slot, side], recv_sem=halo_recv.at[slot, side],
            device_id=(to, c), device_id_type=MESH,
        )

    halos = [[halo_copy(0, side, after), halo_copy(1, side, before)] for side in range(2)]
    for side in (1, 0):
        for copy in halos[side]:
            copy.start()

    w_one = pltpu.make_async_remote_copy(
        src_ref=wown, dst_ref=wgot, send_sem=wone_send, recv_sem=wone_recv,
        device_id=(fr_n, fr_c), device_id_type=MESH,
    )

    def w_copy(r, slot):
        return pltpu.make_async_remote_copy(
            src_ref=wgot, dst_ref=wall.at[slot], send_sem=w_send.at[r], recv_sem=w_recv.at[slot],
            device_id=(turn(r), c), device_id_type=MESH,
        )

    @pl.when(to_other)
    def _():
        w_one.start()

    @pl.when(to_self)
    def _():
        wgot[...] = wown[...]

    small_copies[3].wait()
    taken = shuffle_ref[...]
    at = lax.broadcasted_iota(jnp.int32, taken.shape, 1)
    scale = (65536 + blocks - 1) // blocks
    taken_node, at_node = (taken * scale) >> 16, (at * scale) >> 16
    mine = at_node == n
    for d in range(nodes):
        pick_ref[d] = jnp.max(jnp.where(jnp.logical_and(mine, taken_node == d), at - n * blocks, 0))
    for i in range(blocks):
        from_ref[i] = jnp.max(jnp.where(taken == n * blocks + i, at_node, 0))

    for b in range(reach, blocks - reach):
        band(b)
    for i in range(reach, blocks - reach):
        corrupt[i] = acc[reach + i, width:].astype(BF16)
    for copy in halos[1]:
        copy.wait_recv()
    for i in range(reach):
        corrupt[i] = (acc[reach + i, width:] + halo[0, 1, i].astype(F32)).astype(BF16)
        j = blocks - reach + i
        corrupt[j] = (acc[reach + j, width:] + halo[1, 1, i].astype(F32)).astype(BF16)

    def un_copy(q, r, dest, slot):
        return pltpu.make_async_remote_copy(
            src_ref=outgoing.at[dest, pl.ds(q * part, part)], dst_ref=incoming[q].at[slot],
            send_sem=un_send.at[q, r], recv_sem=un_recv.at[q, slot],
            device_id=(dest, c), device_id_type=MESH,
        )

    @pl.loop(1, nodes)
    def _(r):
        dest = turn(r)
        outgoing[dest] = corrupt[pick_ref[dest]]
        un_copy(0, r, dest, n).start()

    for q in range(1, chunks):

        @pl.loop(1, nodes)
        def _(r):
            un_copy(q, r, turn(r), n).start()

    for q in range(chunks):
        incoming[q][n] = corrupt[pick_ref[n], q * part : (q + 1) * part]

    for copy in halos[0]:
        copy.wait_recv()

    def ring_copy(s, q, to_right):
        shard = 2 * lax.rem(z + (depth - s if to_right else s), depth) + core
        where = gathered.at[shard, pl.ds(q * part, part)]
        return pltpu.make_async_remote_copy(
            src_ref=where, dst_ref=where,
            send_sem=(cw_send if to_right else ccw_send).at[s, q],
            recv_sem=(cw_recv if to_right else ccw_recv).at[s, q],
            device_id=(n, right if to_right else left), device_id_type=MESH,
        )

    def sib_copy(t, zz, q):
        where = gathered.at[2 * zz + core, pl.ds(q * part, part)]
        return pltpu.make_async_remote_copy(
            src_ref=where, dst_ref=where, send_sem=sib_send.at[t, q], recv_sem=sib_recv.at[t, q],
            device_id=(n, sib), device_id_type=MESH,
        )

    def goes(s, q, to_right):
        return s + 1 < half or (s + 1 == half and (q < chunks // 2) == to_right)

    def send_on(s, q, to_right):
        if goes(s, q, to_right):
            ring_copy(s, q, to_right).start()

    def own(q):
        @pl.loop(1, nodes)
        def _(r):
            un_copy(q, r, peer(r), peer(nodes - r)).wait_recv()

        here = slice(q * part, (q + 1) * part)
        for i in range(blocks):
            block = acc[reach + i, here] + incoming[q][from_ref[i]].astype(F32)
            if i < reach:
                block = block + halo[0, 0, i, here].astype(F32)
            if i >= blocks - reach:
                block = block + halo[1, 0, i - (blocks - reach), here].astype(F32)
            gathered[c, here, i * rows : (i + 1) * rows] = block.astype(BF16)
        send_on(0, q, True)
        send_on(0, q, False)
        sib_copy(0, z, q).start()

    def step(s, q):
        if goes(s - 1, q, True):
            ring_copy(s - 1, q, True).wait_recv()
            send_on(s, q, True)
            sib_copy(s, lax.rem(z + depth - s, depth), q).start()
        if goes(s - 1, q, False):
            ring_copy(s - 1, q, False).wait_recv()
            send_on(s, q, False)
            sib_copy(half if s == half else half + s, lax.rem(z + s, depth), q).start()

    low = lax.broadcasted_iota(jnp.int32, wown.shape, 1) < width

    def swap(value):
        return pltpu.roll(value, width, 1)

    def weights():
        @pl.loop(1, nodes)
        def _(r):
            w_copy(r, peer(nodes - r)).wait_recv()

        for zz in range(depth):
            here = slice(2 * width * zz, 2 * width * (zz + 1))
            for h in range(2):
                one = wall[2 * h * depth + zz].astype(F32)
                two = wall[(2 * h + 1) * depth + zz].astype(F32)
                at = 2 * short * h
                wrows[at : at + short, here] = jnp.where(low, one, swap(two)).astype(BF16)
                wrows[at + short : at + 2 * short, here] = jnp.where(low, swap(one), two).astype(BF16)

    def gw_copy(dest, slot):
        return pltpu.make_async_remote_copy(
            src_ref=gw_out.at[dest], dst_ref=gw_in.at[slot], send_sem=gw_send.at[dest], recv_sem=gw_recv.at[slot],
            device_id=(dest, c), device_id_type=MESH,
        )

    def use(zz):
        pair = gathered[pl.ds(2 * zz, 2)].reshape(2 * width, blocks * rows)
        product = lax.dot_general(feat[...], pair, (((1,), (1,)), ((), ())), preferred_element_type=F32)
        for h in range(2):
            top = product[2 * short * h : 2 * short * h + short]
            bottom = product[2 * short * h + short : 2 * short * (h + 1)]
            gw_out[2 * h * depth + zz] = jnp.where(low, top, swap(bottom)).astype(BF16)
            gw_out[(2 * h + 1) * depth + zz] = jnp.where(low, swap(top), bottom).astype(BF16)

    def finish(s):
        sides = (-s, s) if 0 < s < half else (s,)
        for side in sides:
            for q in range(chunks):
                sib_copy(half + s if 0 < side < half else s, z, q).wait_recv()
        count = 4 * len(sides)

        @pl.loop(0, len(sides))
        def _(i):
            use(lax.rem(z + depth - s + 2 * s * i, depth))

        @pl.loop(0, count)
        def _(i):
            j = lax.rem(i + n, count)
            zz = lax.rem(z + depth - s + 2 * s * (j // 4), depth)
            dest = lax.rem(j, 4) * depth + zz

            @pl.when(dest != n)
            def _():
                gw_copy(dest, n).start()

            @pl.when(dest == n)
            def _():
                gw_in[n] = gw_out[n]

    for q in range(chunks):
        own(q)
    for s in range(1, half + 1):
        for q in range(chunks):
            step(s, q)
        if s == 1:
            small_copies[5].wait()

            @pl.when(to_other)
            def _():
                w_one.wait()

            wall[n] = wgot[...]
        if s < half:

            @pl.loop(1 + (nodes - 1) * (s - 1) // (half - 1), 1 + (nodes - 1) * s // (half - 1))
            def _(r):
                w_copy(r, n).start()

        finish(s - 1)
    if half == 1:

        @pl.loop(1, nodes)
        def _(r):
            w_copy(r, n).start()

    finish(half)
    weights()

    @pl.loop(1, nodes)
    def _(r):
        gw_copy(peer(r), peer(nodes - r)).wait_recv()

    gw_sum[...] = jnp.sum(gw_in[...].astype(F32), axis=0)
    last = pltpu.make_async_remote_copy(
        src_ref=gw_sum, dst_ref=gw_last, send_sem=last_send, recv_sem=last_recv,
        device_id=(to_n, to_c), device_id_type=MESH,
    )

    @pl.when(to_other)
    def _():
        last.start()

    tile = 2 * rows
    for at in range(0, blocks * rows, tile):
        sums = gathered[:, :, at : at + tile].reshape(chans * width, tile)
        gf_ref[:, at : at + tile] = jnp.dot(wrows[...], sums, preferred_element_type=F32).astype(BF16)
    gf_copy = pltpu.make_async_copy(gf_ref, gf_hbm, gf_sem)
    gf_copy.start()

    for side in range(2):
        for copy in halos[side]:
            copy.wait_send()

    @pl.loop(1, nodes)
    def _(r):
        w_copy(r, n).wait_send()
        gw_copy(peer(r), n).wait_send()
        for q in range(chunks):
            un_copy(q, r, peer(r), n).wait_send()

    for q in range(chunks):
        for s in range(half):
            for to_right in (True, False):
                if goes(s, q, to_right):
                    ring_copy(s, q, to_right).wait_send()
        for t in range(2 * half):
            sib_copy(t, z, q).wait_send()

    @pl.when(to_self)
    def _():
        gw_last[...] = gw_sum[...]

    @pl.when(to_other)
    def _():
        last.wait()

    piece = gw_last[...]
    gw_ref[:short] = piece[:, :width]
    gw_ref[short:] = swap(piece)[:, :width]
    gf_copy.wait()


def local(
    features, weight, pre_clean, pre_corrupt, grad_clean, grad_corrupt, slopes, adj_vals, adj_cols, adj_count, shuffle_from
):
    nodes, chans = lax.axis_size("node"), lax.axis_size("chan")
    row_count, width = features.shape
    blocks, slots, rows, _ = adj_vals.shape
    reach = (slots - 1) // 2
    half = chans // 4
    chunks = 2
    short = weight.shape[0] // 2
    part = width // chunks
    vmem = pl.BlockSpec(memory_space=pltpu.VMEM)
    hbm = pl.BlockSpec(memory_space=pltpu.HBM)
    dma = pltpu.SemaphoreType.DMA
    gw, gf = pl.pallas_call(
        functools.partial(layer_kernel, chunks),
        out_shape=(
            jax.ShapeDtypeStruct((2 * short, width), F32),
            jax.ShapeDtypeStruct((width, row_count), BF16),
        ),
        in_specs=[hbm] * 11,
        out_specs=(vmem, hbm),
        scratch_shapes=[
            pltpu.VMEM((chans, width, row_count), BF16),
            pltpu.VMEM((width, row_count), BF16),
            pltpu.SMEM((nodes,), jnp.int32),
            pltpu.SMEM((blocks,), jnp.int32),
            pltpu.SMEM((slots, blocks), jnp.int32),
            pltpu.SMEM((blocks,), jnp.int32),
            pltpu.VMEM((1, nodes * blocks), jnp.int32),
            pltpu.VMEM((1, width), F32),
            pltpu.VMEM((4, width, row_count), BF16),
            pltpu.VMEM((blocks, slots, rows, rows), BF16),
            pltpu.VMEM((blocks + 2 * reach, 2 * width, rows), F32),
            pltpu.VMEM((2, reach, 2 * width, rows), BF16),
            pltpu.VMEM((blocks, width, rows), BF16),
            pltpu.VMEM((nodes, width, rows), BF16),
            pltpu.VMEM((2, 2, reach, width, rows), BF16),
            pltpu.VMEM(weight.shape, BF16),
            pltpu.VMEM((short, 2 * width), BF16),
            pltpu.VMEM((short, 2 * width), BF16),
            pltpu.VMEM((nodes, short, 2 * width), BF16),
            pltpu.VMEM((4 * short, chans * width), BF16),
            pltpu.VMEM((width, row_count), BF16),
            pltpu.VMEM((nodes, short, 2 * width), BF16),
            pltpu.VMEM((nodes, short, 2 * width), BF16),
            pltpu.VMEM((short, 2 * width), F32),
            pltpu.VMEM((short, 2 * width), F32),
            dma((4,)),
            dma((blocks,)),
            dma((6,)),
            dma((2, 2)),
            dma((2, 2)),
            dma,
            dma,
            dma((nodes,)),
            dma((nodes,)),
            dma((chunks, nodes)),
            dma((chunks, nodes)),
            dma((half, chunks)),
            dma((half, chunks)),
            dma((half, chunks)),
            dma((half, chunks)),
            dma((2 * half, chunks)),
            dma((2 * half, chunks)),
            dma((nodes,)),
            dma((nodes,)),
            dma,
            dma,
            dma,
        ]
        + [pltpu.VMEM((nodes, part, rows), BF16)] * chunks,
        compiler_params=pltpu.CompilerParams(
            collective_id=0, has_side_effects=True, vmem_limit_bytes=62 * 2**20
        ),
        cost_estimate=pl.CostEstimate(
            flops=4 * row_count * width * width * chans, bytes_accessed=8 * 2**20, transcendentals=0
        ),
        name="layer",
    )(
        adj_cols.T, adj_count, shuffle_from[None, :], grad_clean.T, pre_clean.T, grad_corrupt.T, pre_corrupt.T,
        slopes[None, :], adj_vals, weight, features.T,
    )
    return (gw, gf.T)


def solution(mesh):
    placed = (
        P("node", "chan"),
        P("node", "chan"),
        P("node", "chan"),
        P("node", "chan"),
        P("node", "chan"),
        P("node", "chan"),
        P("chan"),
        P("node", None, None, None),
        P("node", None),
        P("node"),
        P(),
    )
    return jax.shard_map(
        local,
        mesh=mesh,
        in_specs=placed,
        out_specs=(P("node", "chan"), P("node", "chan")),
        check_vma=False,
    )
```
